1024 devices in a mesh: section: 64 (over y, x, z_hi, core), dp: 16 (over z_lo).
Axes of the slice: x: 4, y: 4, z: 32 (z_hi: 2, z_lo: 16; z = z_hi * 16 + z_lo), core: 2. Of those that a mesh axis runs over, the one named last changes fastest.
Arguments:
- patches: bfloat16 [16, 4096, 3200], P('dp', 'section'), may hold values from -6 to 6
- live: int32 [16, 64], P('dp'), may hold values from 1 to 64, 1536 in all within a row
- rounds: int32 [16, 64], P('dp'), may hold values from 0 to 63, each once within a row
- ln_gain: float32 [3200], replicated, may hold values from 0.1 to 1.9
- fc1_weight: bfloat16 [3200, 10240], P(None, 'dp'), may hold values from -0.109375 to 0.109375
- fc1_bias: float32 [10240], P('dp'), may hold values from -3 to 3
- fc2_weight: bfloat16 [10240, 3200], P('dp'), may hold values from -0.0625 to 0.0625
- fc2_bias: float32 [3200], replicated, may hold values from -3 to 3
- layer_scale: float32 [3200], replicated, may hold values from 0.5 to 2
Outputs:
- encoded: bfloat16 [16, 1536, 3200], P('dp', 'section')
The draws below stay inside these ranges and needn't reach their ends.
Inputs may be any that keep to these rules, and one draw needn't show every extreme that they name: In each row d the 64 counts sum to 1536, and some device holds exactly 64 live rows. Each rounds[d] lists every section index exactly once.
All inputs are finite; a program needn't handle non-finite values.
Results may differ from the reference program's by a relative error of at most 0.017.
Values may be sent and summed in bfloat16 or wider, within the bound.
No kernel may reach another device: no remote copies, remote signals or barrier semaphores. Data moves between devices by JAX's collectives and lax.ppermute only.
A program may use at most 32 MiB of HBM per device.

```python
import math
import jax
import jax.numpy as jnp
import numpy as np
from jax import lax

D = 3200
FF = 10240
SLOTS = 64
RMAX = 24
N_SECTION = 64
N_DP = 16


def block_scale(key, shape, shards, least, top_value):
    gain = 1.0
    for dim, blocks in shards:
        heights = jax.random.uniform(jax.random.fold_in(jax.random.fold_in(key, 6), dim), (blocks,), jnp.float32, least / len(shards), top_value / len(shards))
        gain = gain * jnp.repeat(jnp.exp(heights), shape[dim] // blocks).reshape((-1,) + (1,) * (len(shape) - 1 - dim))
    return gain


def length_profile(count, total, most, lean):
    loads = [(1 << 20) // math.isqrt(standing ** lean) + 1 for standing in range(2, count + 1)]
    rest, holding = total - most - (count - 1), [1] * (count - 1)
    while rest > 0:
        free = [i for i in range(count - 1) if holding[i] < most]
        pool, remaining = sum([loads[i] for i in free]), rest
        for i in free:
            addition = min(most - holding[i], max(1, remaining * loads[i] // pool), rest)
            holding[i] = holding[i] + addition
            rest = rest - addition
    return np.array([most] + holding)


def uneven_parts(key, count, total, most, skew):
    if count == 2:
        one = jax.random.randint(key, (), max(1, total - most), min(most, total - 1) + 1)
        return jnp.stack([one, total - one])
    sizes = jnp.asarray(length_profile(count, total, most, skew), jnp.int32)
    couples = (count - 1) // 2
    giver, receiver = sizes[1:1 + 2 * couples:2], sizes[2:2 + 2 * couples:2]
    slack = jnp.minimum(giver - 1, most - receiver)
    moved = jax.random.randint(jax.random.fold_in(key, 1), (couples,), 0, 1 << 20) % (slack + 1)
    sizes = sizes.at[1:1 + 2 * couples:2].set(giver - moved).at[2:2 + 2 * couples:2].set(receiver + moved)
    return sizes[jax.random.permutation(jax.random.fold_in(key, 2), count)]


def gaussian(key, shape, deviation, bound, split=(), kind=jnp.bfloat16):
    drawn = deviation * jax.random.normal(key, shape, jnp.float32)
    if split:
        drawn = drawn * block_scale(key, shape, split, -0.22, 0.18)
    return jnp.clip(drawn, -bound, bound).astype(kind)


def setup_inputs(seed: int = 0) -> dict:
    keys = jax.random.split(jax.random.key(seed), 10)
    patches = gaussian(keys[0], (N_DP, N_SECTION * SLOTS, D), 1.0, 6.0, ((0, 16), (1, 64)))
    live = jax.vmap(lambda own: uneven_parts(own, N_SECTION, N_SECTION * RMAX, SLOTS, 2))(jax.random.split(keys[1], N_DP)).reshape((N_DP, N_SECTION)).astype(jnp.int32)
    rounds = jax.vmap(lambda own: jax.random.permutation(own, N_SECTION))(jax.random.split(keys[2], N_DP)).reshape((N_DP, N_SECTION)).astype(jnp.int32)
    ln_gain = jnp.clip(1.0 + 0.18 * jax.random.normal(keys[3], (D,), jnp.float32), 0.1, 1.9)
    fc1_weight = gaussian(keys[4], (D, FF), D ** -0.5, 0.109375, ((1, 16),))
    fc1_bias = gaussian(keys[5], (FF,), 0.5, 3.0, ((0, 16),), jnp.float32)
    fc2_weight = gaussian(keys[6], (FF, D), FF ** -0.5, 0.0625, ((0, 16),))
    fc2_bias = gaussian(keys[7], (D,), 0.5, 3.0, (), jnp.float32)
    layer_scale = jnp.clip(jnp.exp(jax.random.uniform(keys[8], (D,), jnp.float32, math.log(0.5), math.log(2.0))), 0.5, 2.0)
    return dict(patches=patches, live=live, rounds=rounds, ln_gain=ln_gain, fc1_weight=fc1_weight, fc1_bias=fc1_bias, fc2_weight=fc2_weight, fc2_bias=fc2_bias, layer_scale=layer_scale)


def route_column(patch_col, live_row, order_row):
    ends = jnp.cumsum(live_row)
    starts = ends - live_row
    slot_ids = jnp.arange(SLOTS, dtype=jnp.int32)
    global_row = starts[:, None] + slot_ids[None, :]
    valid = slot_ids[None, :] < live_row[:, None]
    round_ids = jnp.minimum(global_row // N_SECTION, RMAX - 1)
    position = global_row % N_SECTION
    target = order_row[position]
    index = jnp.where(valid, target * RMAX + round_ids, N_SECTION * RMAX).reshape(-1).astype(jnp.int32)
    empty = jnp.zeros((N_SECTION * RMAX, D), jnp.bfloat16)
    return empty.at[index].set(patch_col, mode='drop')

def encode_column(args):
    patch_col, live_row, order_row, ln_gain, fc1_weight, fc1_bias, fc2_weight, fc2_bias, layer_scale = args
    routed = route_column(patch_col, live_row, order_row)
    rows32 = routed.astype(jnp.float32)
    mean = lax.optimization_barrier(jnp.mean(rows32, axis=1, keepdims=True))
    centered = rows32 - mean
    var = lax.optimization_barrier(jnp.mean(centered * centered, axis=1, keepdims=True))
    normed = (centered * lax.rsqrt(var + 1e-06) * ln_gain).astype(jnp.bfloat16)
    pre = jnp.dot(normed, fc1_weight, preferred_element_type=jnp.float32) + fc1_bias
    hidden = jax.nn.gelu(pre, approximate=False).astype(jnp.bfloat16)
    group = FF // N_DP
    hidden_groups = hidden.reshape(N_SECTION * RMAX, N_DP, group).transpose(1, 0, 2)
    weight_groups = fc2_weight.reshape(N_DP, group, D)

    def one_group(pair):
        return jnp.dot(pair[0], pair[1], preferred_element_type=jnp.float32).astype(jnp.bfloat16)
    parts = lax.map(one_group, (hidden_groups, weight_groups))
    summed = lax.optimization_barrier(jnp.sum(parts.astype(jnp.float32), axis=0))
    return (rows32 + layer_scale * (summed + fc2_bias)).astype(jnp.bfloat16)

def reference(patches, live, rounds, ln_gain, fc1_weight, fc1_bias, fc2_weight, fc2_bias, layer_scale):
    outputs = []
    for column in range(N_DP):
        outputs.append(encode_column((patches[column], live[column], rounds[column], ln_gain, fc1_weight, fc1_bias, fc2_weight, fc2_bias, layer_scale)))
    return jnp.stack(outputs, axis=0)
```

```python
import jax
import jax.numpy as jnp
from jax import lax
from jax.sharding import PartitionSpec as P

AXES = ("section", "dp")


def coordinates(sections, dps):
    for section in range(sections):
        for dp in range(dps):
            yield section // 4, (section // 2 % 2) * dps + dp, section % 2, section * dps + dp


def shift_pairs(sections, dps, hops):
    ring = 2 * dps
    pairs = []
    for column, z, core, flat in coordinates(sections, dps):
        there = (z + (hops if core == 0 else -hops)) % ring
        section = (column * 2 + there // dps) * 2 + core
        pairs.append((flat, section * dps + there % dps))
    return pairs


def swap_pairs(sections, dps):
    return [(s * dps + d, (s ^ 1) * dps + d) for s in range(sections) for d in range(dps)]


def route(patches, live_row, order_row, my_section, section_count, keep_rows):
    slot_count = patches.shape[0]
    width = patches.shape[1]
    section_ids = jnp.arange(section_count, dtype=jnp.int32)
    ends = jnp.cumsum(live_row)
    starts = ends - live_row
    is_mine = section_ids == my_section
    my_start = jnp.sum(jnp.where(is_mine, starts, 0))
    my_live = jnp.sum(jnp.where(is_mine, live_row, 0))
    slot_ids = jnp.arange(slot_count, dtype=jnp.int32)
    position = (my_start + slot_ids) % section_count
    target = jnp.sum(
        jnp.where(position[:, None] == section_ids[None, :], order_row[None, :], 0), axis=1
    )
    send_index = jnp.where(slot_ids < my_live, target, section_count)
    send_rows = (
        jnp.zeros((section_count, width), jnp.bfloat16).at[send_index].set(patches, mode="drop")
    )
    received = lax.all_to_all(send_rows, "section", split_axis=0, concat_axis=0, tiled=True)
    my_position = jnp.sum(jnp.where(order_row == my_section, section_ids, 0))
    keep_ids = jnp.arange(keep_rows, dtype=jnp.int32)
    row_global = keep_ids * section_count + my_position
    source_ids = jnp.sum((ends[None, :] <= row_global[:, None]).astype(jnp.int32), axis=1)
    return received[source_ids]


def per_device(
    patches, live, rounds, ln_gain, fc1_weight, fc1_bias, fc2_weight, fc2_bias, layer_scale
):
    sections = lax.axis_size("section")
    dps = lax.axis_size("dp")
    my_section = lax.axis_index("section")
    up = my_section % 2 == 0
    keep_rows = 3 * sections // 8

    def send(value, hops):
        return lax.ppermute(value, AXES, shift_pairs(sections, dps, hops))

    def swap(value):
        return lax.ppermute(value, AXES, swap_pairs(sections, dps))

    routed = route(patches[0], live[0], rounds[0], my_section, sections, keep_rows)
    rows32 = routed.astype(jnp.float32)
    mean = jnp.mean(rows32, axis=1, keepdims=True)
    centered = rows32 - mean
    var = jnp.mean(centered * centered, axis=1, keepdims=True)
    normed = (centered * lax.rsqrt(var + 1e-06) * ln_gain).astype(jnp.bfloat16)
    other = swap(normed)
    even = jnp.where(up, normed, other)
    odd = jnp.where(up, other, normed)

    def gather(own):
        far3 = send(own, 3)
        far6 = send(far3, 3)
        level0 = jnp.concatenate([own, far3, far6], axis=0)
        level1 = send(level0, 1)
        level2 = send(level1, 1)
        return level0, level1, level2

    def encode(levels):
        level0, level1, level2 = levels
        n = level0.shape[0] // 3
        ends = jnp.where(up, level2[2 * n :], level0[:n])
        rows = jnp.concatenate([level0[n:], level1, level2[: 2 * n], ends], axis=0)
        pre = jnp.dot(rows, fc1_weight, preferred_element_type=jnp.float32) + fc1_bias
        hidden = jax.nn.gelu(pre, approximate=False).astype(jnp.bfloat16)
        return jnp.dot(hidden, fc2_weight, preferred_element_type=jnp.float32).astype(jnp.bfloat16)

    def scatter(part):
        n = part.shape[0] // 8
        ends = part[7 * n :]
        none = jnp.zeros_like(ends)
        sum0 = jnp.concatenate([jnp.where(up, none, ends), part[: 2 * n]], axis=0)
        sum1 = part[2 * n : 5 * n]
        sum2 = jnp.concatenate([part[5 * n : 7 * n], jnp.where(up, ends, none)], axis=0)

        def add(a, b):
            return (a.astype(jnp.float32) + b.astype(jnp.float32)).astype(jnp.bfloat16)

        total = add(send(sum2, -1), sum1)
        total = add(send(total, -1), sum0)
        back = add(send(total[2 * n :], -3), total[n : 2 * n])
        return add(send(back, -3), total[:n])

    sum_even = scatter(encode(gather(even)))
    sum_odd = scatter(encode(gather(odd)))

    mine = jnp.where(up, sum_even, sum_odd)
    theirs = jnp.where(up, sum_odd, sum_even)
    summed = mine.astype(jnp.float32) + swap(theirs).astype(jnp.float32)
    encoded = (rows32 + layer_scale * (summed + fc2_bias)).astype(jnp.bfloat16)
    return encoded[None]


def solution(mesh):
    placed = (
        P("dp", "section", None),
        P("dp", None),
        P("dp", None),
        P(),
        P(None, "dp"),
        P("dp"),
        P("dp", None),
        P(),
        P(),
    )
    return jax.shard_map(
        per_device, mesh=mesh, in_specs=placed, out_specs=P("dp", "section", None), check_vma=False
    )
```

```python
import jax
import jax.numpy as jnp
from jax import lax
from jax.experimental import pallas as pl
from jax.experimental.pallas import tpu as pltpu
from jax.sharding import PartitionSpec as P

AXES = ("section", "dp")


def shift_pairs(sections, dps, hops):
    ring = 2 * dps
    pairs = []
    for section in range(sections):
        for dp in range(dps):
            there = (section // 2 % 2 * dps + dp + hops) % ring
            target = (section // 4 * 2 + there // dps) * 2 + section % 2
            pairs.append((section * dps + dp, target * dps + there % dps))
    return pairs


def half_groups(sections):
    return [[s for s in range(sections) if s // 2 % 2 == half] for half in range(2)]


def plan_kernel(mine_ref, live_ref, order_ref, patches_ref, far_ref, near_ref, pick_far_ref, pick_near_ref):
    sections = live_ref.shape[1]
    half = sections // 2
    keep = pick_far_ref.shape[0]
    mine = mine_ref[0]
    my_half = mine // 2 % 2
    live = live_ref[...].astype(jnp.float32)
    order = order_ref[...]
    down = lax.broadcasted_iota(jnp.int32, (sections, sections), 0)
    along = lax.broadcasted_iota(jnp.int32, (sections, sections), 1)
    live_down = jnp.sum(jnp.where(down == along, live, 0.0), axis=1, keepdims=True)
    starts_down = jnp.sum(jnp.where(along < down, live, 0.0), axis=1, keepdims=True)
    is_me = lax.broadcasted_iota(jnp.int32, (sections, 1), 0) == mine
    my_start = jnp.sum(jnp.where(is_me, starts_down, 0.0), axis=0, keepdims=True)
    my_live = jnp.sum(jnp.where(is_me, live_down, 0.0), axis=0, keepdims=True)
    peer = down % half
    toward = jnp.where(down < half, 1 - my_half, my_half)
    target = peer // 2 * 4 + toward * 2 + peer % 2
    place = jnp.sum(jnp.where(order == target, along, 0).astype(jnp.float32), axis=1, keepdims=True)
    slot = (place - my_start).astype(jnp.int32) & (sections - 1)
    wanted = (along == slot) & (slot.astype(jnp.float32) < my_live)
    move = jnp.where(wanted, 1.0, 0.0).astype(jnp.bfloat16)
    sent = jnp.dot(move, patches_ref[...], preferred_element_type=jnp.float32).astype(jnp.bfloat16)
    far_ref[...] = sent[:half]
    near_ref[...] = sent[half:]
    peers = lax.broadcasted_iota(jnp.int32, (sections, half), 1)
    source = peers // 2 * 4 + my_half * 2 + peers % 2
    from_it = lax.broadcasted_iota(jnp.int32, (sections, half), 0) == source
    first = jnp.sum(jnp.where(from_it, starts_down, 0.0), axis=0, keepdims=True)
    last = first + jnp.sum(jnp.where(from_it, live_down, 0.0), axis=0, keepdims=True)
    rounds = lax.broadcasted_iota(jnp.int32, (keep, half), 0) * sections
    lanes = lax.broadcasted_iota(jnp.int32, (1, sections), 1)
    for owner, pick_ref in ((mine ^ 2, pick_far_ref), (mine, pick_near_ref)):
        at = jnp.sum(jnp.where(order == owner, lanes, 0).astype(jnp.float32), axis=1, keepdims=True)
        number = rounds.astype(jnp.float32) + at
        pick_ref[...] = jnp.where((number >= first) & (number < last), 1.0, 0.0).astype(jnp.bfloat16)


def plan(patches, live, order, mine, keep):
    slots, width = patches.shape
    half = live.shape[1] // 2
    vmem = pl.BlockSpec(memory_space=pltpu.VMEM)
    return pl.pallas_call(
        plan_kernel,
        out_shape=(
            jax.ShapeDtypeStruct((half, width), jnp.bfloat16),
            jax.ShapeDtypeStruct((half, width), jnp.bfloat16),
            jax.ShapeDtypeStruct((keep, half), jnp.bfloat16),
            jax.ShapeDtypeStruct((keep, half), jnp.bfloat16),
        ),
        in_specs=[pl.BlockSpec(memory_space=pltpu.SMEM), vmem, vmem, vmem],
        out_specs=(vmem, vmem, vmem, vmem),
        compiler_params=pltpu.CompilerParams(vmem_limit_bytes=16 * 1024 * 1024),
    )(mine[None], live, order, patches)


def pick(chosen, rows):
    return jnp.dot(chosen, rows, preferred_element_type=jnp.float32).astype(jnp.bfloat16)


def per_device(
    patches, live, rounds, ln_gain, fc1_weight, fc1_bias, fc2_weight, fc2_bias, layer_scale
):
    sections = lax.axis_size("section")
    dps = lax.axis_size("dp")
    mine = lax.axis_index("section").astype(jnp.int32)
    keep_rows = 3 * sections // 8
    groups = half_groups(sections)

    def exchange(rows):
        return lax.all_to_all(
            rows, "section", split_axis=0, concat_axis=0, axis_index_groups=groups, tiled=True
        )

    far, near, pick_far, pick_near = plan(patches[0], live, rounds, mine, keep_rows)
    crossing = pick(pick_far, exchange(far))
    crossed = lax.ppermute(crossing, AXES, shift_pairs(sections, dps, dps))
    crossing, near = lax.optimization_barrier((crossing, near))
    stayed = pick(pick_near, exchange(near))
    routed = stayed + crossed

    return finish(
        routed, sections, dps, ln_gain, fc1_weight, fc1_bias, fc2_weight, fc2_bias, layer_scale
    )


def finish(routed, sections, dps, ln_gain, fc1_weight, fc1_bias, fc2_weight, fc2_bias, layer_scale):
    keep = routed.shape[0]

    def send(value, hops):
        return lax.ppermute(value, AXES, shift_pairs(sections, dps, hops))

    def encode(rows):
        pre = jnp.dot(rows, fc1_weight, preferred_element_type=jnp.float32) + fc1_bias
        hidden = jax.nn.gelu(pre, approximate=False).astype(jnp.bfloat16)
        return jnp.dot(hidden, fc2_weight, preferred_element_type=jnp.float32).astype(jnp.bfloat16)

    def add(a, b):
        return (a.astype(jnp.float32) + b.astype(jnp.float32)).astype(jnp.bfloat16)

    rows32 = routed.astype(jnp.float32)
    mean = jnp.mean(rows32, axis=1, keepdims=True)
    centered = rows32 - mean
    var = jnp.mean(centered * centered, axis=1, keepdims=True)
    normed = (centered * lax.rsqrt(var + 1e-06) * ln_gain).astype(jnp.bfloat16)

    up3, down3 = send(normed, 3), send(normed, -3)
    up6, down6 = send(up3, 3), send(down3, -3)
    up036 = jnp.concatenate([normed, up3, up6], axis=0)
    down036 = jnp.concatenate([normed, down3, down6], axis=0)
    up147, down147 = send(up036, 1), send(down036, -1)
    up258, down25 = send(up147, 1), send(down147[: 2 * keep], -1)

    part0 = encode(jnp.concatenate([up036[keep:], down036], axis=0))
    part1 = encode(jnp.concatenate([up147, down147], axis=0))
    part2 = encode(jnp.concatenate([up258, down25], axis=0))

    none = jnp.zeros((keep, routed.shape[1]), jnp.bfloat16)
    up_sum = add(send(part2[: 3 * keep], -1), part1[: 3 * keep])
    down_sum = add(
        jnp.concatenate([send(part2[3 * keep :], 1), none], axis=0), part1[3 * keep :]
    )
    up_sum = add(send(up_sum, -1), jnp.concatenate([none, part0[: 2 * keep]], axis=0))
    down_sum = add(send(down_sum, 1), part0[2 * keep :])
    up_back = add(send(up_sum[2 * keep :], -3), up_sum[keep : 2 * keep])
    down_back = add(send(down_sum[2 * keep :], 3), down_sum[keep : 2 * keep])
    up_home, down_home = send(up_back, -3), send(down_back, 3)
    summed = (up_home.astype(jnp.float32) + up_sum[:keep].astype(jnp.float32)) + (
        down_home.astype(jnp.float32) + down_sum[:keep].astype(jnp.float32)
    )
    return (rows32 + layer_scale * (summed + fc2_bias)).astype(jnp.bfloat16)[None]


def solution(mesh):
    placed = (
        P("dp", "section", None),
        P("dp", None),
        P("dp", None),
        P(),
        P(None, "dp"),
        P("dp"),
        P("dp", None),
        P(),
        P(),
    )
    return jax.shard_map(
        per_device, mesh=mesh, in_specs=placed, out_specs=P("dp", "section", None), check_vma=False
    )
```

```python
import jax
import jax.numpy as jnp
from jax import lax
from jax.experimental import pallas as pl
from jax.experimental.pallas import tpu as pltpu
from jax.sharding import PartitionSpec as P

AXES = ("section", "dp")


def shift_pairs(sections, dps, hops):
    ring = 2 * dps
    pairs = []
    for section in range(sections):
        for dp in range(dps):
            there = (section // 2 % 2 * dps + dp + hops) % ring
            target = (section // 4 * 2 + there // dps) * 2 + section % 2
            pairs.append((section * dps + dp, target * dps + there % dps))
    return pairs


def opposite_pairs(sections, dps, hops):
    up, down = shift_pairs(sections, dps, hops), shift_pairs(sections, dps, -hops)
    return [up[i] if i // dps % 2 == 0 else down[i] for i in range(sections * dps)]


def half_groups(sections):
    return [[s for s in range(sections) if s // 2 % 2 == half] for half in range(2)]


def plan_kernel(mine_ref, live_ref, order_ref, patches_ref, rows_ref, pick_far_ref, pick_near_ref):
    sections = live_ref.shape[1]
    keep = pick_far_ref.shape[0]
    mine = mine_ref[0]
    my_half = mine // 2 % 2
    live = live_ref[...].astype(jnp.float32)
    order = order_ref[...]
    down = lax.broadcasted_iota(jnp.int32, (sections, sections), 0)
    along = lax.broadcasted_iota(jnp.int32, (sections, sections), 1)
    live_down = jnp.sum(jnp.where(down == along, live, 0.0), axis=1, keepdims=True)
    starts_down = jnp.sum(jnp.where(along < down, live, 0.0), axis=1, keepdims=True)
    is_me = lax.broadcasted_iota(jnp.int32, (sections, 1), 0) == mine
    my_start = jnp.sum(jnp.where(is_me, starts_down, 0.0), axis=0, keepdims=True)
    my_live = jnp.sum(jnp.where(is_me, live_down, 0.0), axis=0, keepdims=True)
    peer = down // 2
    toward = jnp.where(down % 2 == 0, 1 - my_half, my_half)
    target = peer // 2 * 4 + toward * 2 + peer % 2
    place = jnp.sum(jnp.where(order == target, along, 0).astype(jnp.float32), axis=1, keepdims=True)
    slot = (place - my_start).astype(jnp.int32) & (sections - 1)
    wanted = (along == slot) & (slot.astype(jnp.float32) < my_live)
    move = jnp.where(wanted, 1.0, 0.0).astype(jnp.bfloat16)
    rows_ref[...] = jnp.dot(
        move, patches_ref[...], preferred_element_type=jnp.float32
    ).astype(jnp.bfloat16)
    lane = lax.broadcasted_iota(jnp.int32, (sections, sections), 1)
    source = lane // 4 * 4 + my_half * 2 + lane // 2 % 2
    from_it = down == source
    first = jnp.sum(jnp.where(from_it, starts_down, 0.0), axis=0, keepdims=True)
    last = first + jnp.sum(jnp.where(from_it, live_down, 0.0), axis=0, keepdims=True)
    rounds = lax.broadcasted_iota(jnp.int32, (keep, sections), 0) * sections
    lanes = lax.broadcasted_iota(jnp.int32, (1, sections), 1)
    for parity, owner, pick_ref in ((0, mine ^ 2, pick_far_ref), (1, mine, pick_near_ref)):
        at = jnp.sum(jnp.where(order == owner, lanes, 0).astype(jnp.float32), axis=1, keepdims=True)
        number = rounds.astype(jnp.float32) + at
        held = (number >= first) & (number < last) & (lanes % 2 == parity)
        pick_ref[...] = jnp.where(held, 1.0, 0.0).astype(jnp.bfloat16)


def plan(patches, live, order, mine, keep):
    slots, width = patches.shape
    vmem = pl.BlockSpec(memory_space=pltpu.VMEM)
    return pl.pallas_call(
        plan_kernel,
        out_shape=(
            jax.ShapeDtypeStruct((slots, width), jnp.bfloat16),
            jax.ShapeDtypeStruct((keep, slots), jnp.bfloat16),
            jax.ShapeDtypeStruct((keep, slots), jnp.bfloat16),
        ),
        in_specs=[pl.BlockSpec(memory_space=pltpu.SMEM), vmem, vmem, vmem],
        out_specs=(vmem, vmem, vmem),
        compiler_params=pltpu.CompilerParams(vmem_limit_bytes=16 * 1024 * 1024),
    )(mine[None], live, order, patches)


def pick(chosen, rows):
    return jnp.dot(chosen, rows, preferred_element_type=jnp.float32).astype(jnp.bfloat16)


def per_device(
    patches, live, rounds, ln_gain, fc1_weight, fc1_bias, fc2_weight, fc2_bias, layer_scale
):
    sections = lax.axis_size("section")
    dps = lax.axis_size("dp")
    mine = lax.axis_index("section").astype(jnp.int32)
    keep = 3 * sections // 8
    groups = half_groups(sections)
    width, units = fc1_weight.shape
    f32 = jnp.float32

    def send(value, hops):
        return lax.ppermute(value, AXES, shift_pairs(sections, dps, hops))

    pieces = sections // 4
    depth = units // pieces
    first = (mine >> 2) * depth
    upper = (mine & 1) == 0
    chosen = first + lax.broadcasted_iota(jnp.int32, (depth, units), 0)
    chosen = (chosen == lax.broadcasted_iota(jnp.int32, (depth, units), 1)).astype(jnp.bfloat16)
    piece1 = lax.dot_general(
        chosen, fc1_weight, (((1,), (1,)), ((), ())), preferred_element_type=f32
    ).astype(jnp.bfloat16)
    piece2 = lax.dynamic_slice_in_dim(fc2_weight, first, depth, axis=0)
    piece = lax.ppermute(
        jnp.where(upper, piece1, piece2), AXES, opposite_pairs(sections, dps, dps // 2)
    )
    rows, pick_far, pick_near = plan(patches[0], live, rounds, mine, keep)
    rows = lax.all_to_all(
        rows, "section", split_axis=0, concat_axis=0, axis_index_groups=groups, tiled=True
    )
    piece = lax.optimization_barrier((piece, rows))[0]
    away_bias = send(fc1_bias, dps // 2)
    fetched = lax.all_gather(
        piece, "section", axis=0, axis_index_groups=groups, tiled=True
    ).reshape(pieces, 2, depth, width)
    away1 = fetched[:, 0].reshape(units, width)
    away2 = fetched[:, 1].reshape(units, width)
    routed = pick(pick_near, rows) + send(pick(pick_far, rows), dps)

    rows32 = routed.astype(f32)
    mean = jnp.mean(rows32, axis=1, keepdims=True)
    centered = rows32 - mean
    var = jnp.mean(centered * centered, axis=1, keepdims=True)
    normed = (centered * lax.rsqrt(var + 1e-06) * ln_gain).astype(jnp.bfloat16)

    up2, down2 = send(normed, 2), send(normed, -2)
    up13 = send(jnp.concatenate([normed, up2], axis=0), 1)
    down13 = send(jnp.concatenate([normed, down2], axis=0), -1)
    up4 = send(up2, 2)
    blocks = jnp.concatenate([up13, up2, up4, down13, down2, normed], axis=0)

    pre = jnp.dot(blocks, fc1_weight, preferred_element_type=f32) + fc1_bias
    hidden = jax.nn.gelu(pre, approximate=False).astype(jnp.bfloat16)
    part = jnp.dot(hidden, fc2_weight, preferred_element_type=f32)
    pre = lax.dot_general(
        blocks, away1, (((1,), (1,)), ((), ())), preferred_element_type=f32
    ) + away_bias
    hidden = jax.nn.gelu(pre, approximate=False).astype(jnp.bfloat16)
    part = (part + jnp.dot(hidden, away2, preferred_element_type=f32)).astype(jnp.bfloat16)

    def add(*parts):
        return sum(p.astype(f32) for p in parts)

    up02 = send(part[: 2 * keep], -1)
    up_far = send(part[3 * keep : 4 * keep], -2)
    down02 = send(part[4 * keep : 6 * keep], 1)
    up_sum = add(part[2 * keep : 3 * keep], up02[keep:], up_far).astype(jnp.bfloat16)
    down_sum = add(part[6 * keep : 7 * keep], down02[keep:]).astype(jnp.bfloat16)
    summed = add(send(up_sum, -2), up02[:keep], send(down_sum, 2), down02[:keep], part[7 * keep :])
    encoded = (rows32 + layer_scale * (summed + fc2_bias)).astype(jnp.bfloat16)
    return encoded[None]


def solution(mesh):
    placed = (
        P("dp", "section", None),
        P("dp", None),
        P("dp", None),
        P(),
        P(None, "dp"),
        P("dp"),
        P("dp", None),
        P(),
        P(),
    )
    return jax.shard_map(
        per_device, mesh=mesh, in_specs=placed, out_specs=P("dp", "section", None), check_vma=False
    )
```

```python
import jax
import jax.numpy as jnp
import numpy as np
from jax import lax
from jax.experimental import pallas as pl
from jax.experimental.pallas import tpu as pltpu
from jax.sharding import PartitionSpec as P

AXES = ("section", "dp")


def shift_pairs(sections, dps, hops):
    ring = 2 * dps
    pairs = []
    for section in range(sections):
        for dp in range(dps):
            there = (section // 2 % 2 * dps + dp + hops) % ring
            target = (section // 4 * 2 + there // dps) * 2 + section % 2
            pairs.append((section * dps + dp, target * dps + there % dps))
    return pairs


def opposite_pairs(sections, dps, hops):
    up, down = shift_pairs(sections, dps, hops), shift_pairs(sections, dps, -hops)
    return [up[i] if i // dps % 2 == 0 else down[i] for i in range(sections * dps)]


def half_groups(sections):
    return [[s for s in range(sections) if s // 2 % 2 == half] for half in range(2)]


def plan_kernel(mine_ref, live_ref, order_ref, patches_ref, rows_ref, pick_far_ref, pick_near_ref):
    sections = live_ref.shape[1]
    keep = pick_far_ref.shape[0]
    mine = mine_ref[0]
    my_half = mine // 2 % 2
    live = live_ref[...].astype(jnp.float32)
    order = order_ref[...]
    down = lax.broadcasted_iota(jnp.int32, (sections, sections), 0)
    along = lax.broadcasted_iota(jnp.int32, (sections, sections), 1)
    live_down = jnp.sum(jnp.where(down == along, live, 0.0), axis=1, keepdims=True)
    starts_down = jnp.sum(jnp.where(along < down, live, 0.0), axis=1, keepdims=True)
    is_me = lax.broadcasted_iota(jnp.int32, (sections, 1), 0) == mine
    my_start = jnp.sum(jnp.where(is_me, starts_down, 0.0), axis=0, keepdims=True)
    my_live = jnp.sum(jnp.where(is_me, live_down, 0.0), axis=0, keepdims=True)
    peer = down // 2
    toward = jnp.where(down % 2 == 0, 1 - my_half, my_half)
    target = peer // 2 * 4 + toward * 2 + peer % 2
    place = jnp.sum(jnp.where(order == target, along, 0).astype(jnp.float32), axis=1, keepdims=True)
    slot = (place - my_start).astype(jnp.int32) & (sections - 1)
    wanted = (along == slot) & (slot.astype(jnp.float32) < my_live)
    move = jnp.where(wanted, 1.0, 0.0).astype(jnp.bfloat16)
    rows_ref[...] = jnp.dot(
        move, patches_ref[...], preferred_element_type=jnp.float32
    ).astype(jnp.bfloat16)
    lane = lax.broadcasted_iota(jnp.int32, (sections, sections), 1)
    source = lane // 4 * 4 + my_half * 2 + lane // 2 % 2
    from_it = down == source
    first = jnp.sum(jnp.where(from_it, starts_down, 0.0), axis=0, keepdims=True)
    last = first + jnp.sum(jnp.where(from_it, live_down, 0.0), axis=0, keepdims=True)
    rounds = lax.broadcasted_iota(jnp.int32, (keep, sections), 0) * sections
    lanes = lax.broadcasted_iota(jnp.int32, (1, sections), 1)
    for parity, owner, pick_ref in ((0, mine ^ 2, pick_far_ref), (1, mine, pick_near_ref)):
        at = jnp.sum(jnp.where(order == owner, lanes, 0).astype(jnp.float32), axis=1, keepdims=True)
        number = rounds.astype(jnp.float32) + at
        held = (number >= first) & (number < last) & (lanes % 2 == parity)
        pick_ref[...] = jnp.where(held, 1.0, 0.0).astype(jnp.bfloat16)


def plan(patches, live, order, mine, keep):
    slots, width = patches.shape
    vmem = pl.BlockSpec(memory_space=pltpu.VMEM)
    return pl.pallas_call(
        plan_kernel,
        out_shape=(
            jax.ShapeDtypeStruct((slots, width), jnp.bfloat16),
            jax.ShapeDtypeStruct((keep, slots), jnp.bfloat16),
            jax.ShapeDtypeStruct((keep, slots), jnp.bfloat16),
        ),
        in_specs=[pl.BlockSpec(memory_space=pltpu.SMEM), vmem, vmem, vmem],
        out_specs=(vmem, vmem, vmem),
        compiler_params=pltpu.CompilerParams(vmem_limit_bytes=16 * 1024 * 1024),
    )(mine[None], live, order, patches)


def away_kernel(rows_ref, part_ref, bias_ref, fetched_ref, out_ref, w1, w2, hidden, sems):
    units, width = w1.shape
    first = pltpu.make_async_copy(fetched_ref.at[pl.ds(0, units)], w1, sems.at[0])
    second = pltpu.make_async_copy(fetched_ref.at[pl.ds(units, units)], w2, sems.at[1])
    first.start()
    second.start()
    first.wait()
    for at in range(0, units, 256):
        span = pl.ds(at, min(256, units - at))
        pre = lax.dot_general(
            rows_ref[...], w1[span], (((1,), (1,)), ((), ())), preferred_element_type=jnp.float32
        ) + bias_ref[:, span]
        hidden[:, span] = (0.5 * pre * (1.0 + lax.erf(pre * np.float32(0.5**0.5)))).astype(jnp.bfloat16)
    second.wait()
    for at in range(0, width, 640):
        span = pl.ds(at, min(640, width - at))
        out = jnp.dot(hidden[...], w2[:, span], preferred_element_type=jnp.float32)
        out_ref[:, span] = (part_ref[:, span] + out).astype(jnp.bfloat16)


def add_away(rows, part, bias, fetched):
    count, width = rows.shape
    units = bias.shape[0]
    vmem = pl.BlockSpec(memory_space=pltpu.VMEM)
    return pl.pallas_call(
        away_kernel,
        out_shape=jax.ShapeDtypeStruct((count, width), jnp.bfloat16),
        in_specs=[vmem, vmem, vmem, pl.BlockSpec(memory_space=pl.ANY)],
        out_specs=vmem,
        scratch_shapes=[
            pltpu.VMEM((units, width), jnp.bfloat16),
            pltpu.VMEM((units, width), jnp.bfloat16),
            pltpu.VMEM((count, units), jnp.bfloat16),
            pltpu.SemaphoreType.DMA((2,)),
        ],
        compiler_params=pltpu.CompilerParams(vmem_limit_bytes=28 * 1024 * 1024),
    )(rows, part, bias[None], fetched)


def pick(chosen, rows):
    return jnp.dot(chosen, rows, preferred_element_type=jnp.float32).astype(jnp.bfloat16)


def per_device(
    patches, live, rounds, ln_gain, fc1_weight, fc1_bias, fc2_weight, fc2_bias, layer_scale
):
    sections = lax.axis_size("section")
    dps = lax.axis_size("dp")
    mine = lax.axis_index("section").astype(jnp.int32)
    keep = 3 * sections // 8
    groups = half_groups(sections)
    width, units = fc1_weight.shape
    f32 = jnp.float32

    def send(value, hops):
        return lax.ppermute(value, AXES, shift_pairs(sections, dps, hops))

    pieces = sections // 4
    depth = units // pieces
    member = (mine >> 2) * 2 + (mine & 1)
    first = (member & (pieces - 1)) * depth
    upper = member < pieces
    chosen = first + lax.broadcasted_iota(jnp.int32, (depth, units), 0)
    chosen = (chosen == lax.broadcasted_iota(jnp.int32, (depth, units), 1)).astype(jnp.bfloat16)
    piece1 = lax.dot_general(
        chosen, fc1_weight, (((1,), (1,)), ((), ())), preferred_element_type=f32
    ).astype(jnp.bfloat16)
    piece2 = lax.dynamic_slice_in_dim(fc2_weight, first, depth, axis=0)
    piece = jnp.where(upper, piece1, piece2)
    rows, pick_far, pick_near = plan(patches[0], live, rounds, mine, keep)
    piece, rows = lax.optimization_barrier((piece, rows))
    piece = lax.ppermute(piece, AXES, opposite_pairs(sections, dps, dps // 2))
    rows = lax.all_to_all(
        rows, "section", split_axis=0, concat_axis=0, axis_index_groups=groups, tiled=True
    )
    piece = lax.optimization_barrier((piece, rows))[0]
    fetched = lax.all_gather(piece, "section", axis=0, axis_index_groups=groups, tiled=True)
    crossing = pick(pick_far, rows)
    bias = lax.optimization_barrier((fc1_bias, crossing))[0]
    away_bias = send(bias, dps // 2)
    crossed, away_bias = lax.optimization_barrier((send(crossing, dps), away_bias))
    routed = pick(pick_near, rows) + crossed

    rows32 = routed.astype(f32)
    mean = jnp.mean(rows32, axis=1, keepdims=True)
    centered = rows32 - mean
    var = jnp.mean(centered * centered, axis=1, keepdims=True)
    normed = (centered * lax.rsqrt(var + 1e-06) * ln_gain).astype(jnp.bfloat16)

    up2, down2 = send(normed, 2), send(normed, -2)
    up13 = send(jnp.concatenate([normed, up2], axis=0), 1)
    down13 = send(jnp.concatenate([normed, down2], axis=0), -1)
    up4 = send(up2, 2)
    blocks = jnp.concatenate([up13, up2, up4, down13, down2, normed], axis=0)

    pre = jnp.dot(blocks, fc1_weight, preferred_element_type=f32) + fc1_bias
    hidden = jax.nn.gelu(pre, approximate=False).astype(jnp.bfloat16)
    part = jnp.dot(hidden, fc2_weight, preferred_element_type=f32)
    part = add_away(blocks, part, away_bias, fetched)

    def add(*parts):
        return sum(p.astype(f32) for p in parts)

    up02 = send(part[: 2 * keep], -1)
    up_far = send(part[3 * keep : 4 * keep], -2)
    down02 = send(part[4 * keep : 6 * keep], 1)
    up_sum = add(part[2 * keep : 3 * keep], up02[keep:], up_far).astype(jnp.bfloat16)
    down_sum = add(part[6 * keep : 7 * keep], down02[keep:]).astype(jnp.bfloat16)
    summed = add(send(up_sum, -2), up02[:keep], send(down_sum, 2), down02[:keep], part[7 * keep :])
    encoded = (rows32 + layer_scale * (summed + fc2_bias)).astype(jnp.bfloat16)
    return encoded[None]


def solution(mesh):
    placed = (
        P("dp", "section", None),
        P("dp", None),
        P("dp", None),
        P(),
        P(None, "dp"),
        P("dp"),
        P("dp", None),
        P(),
        P(),
    )
    return jax.shard_map(
        per_device, mesh=mesh, in_specs=placed, out_specs=P("dp", "section", None), check_vma=False
    )
```

```python
import jax
import jax.numpy as jnp
import numpy as np
from jax import lax
from jax.experimental import pallas as pl
from jax.experimental.pallas import tpu as pltpu
from jax.sharding import PartitionSpec as P

AXES = ("section", "dp")


def shift_pairs(sections, dps, hops):
    ring = 2 * dps
    pairs = []
    for section in range(sections):
        for dp in range(dps):
            there = (section // 2 % 2 * dps + dp + hops) % ring
            target = (section // 4 * 2 + there // dps) * 2 + section % 2
            pairs.append((section * dps + dp, target * dps + there % dps))
    return pairs


def opposite_pairs(sections, dps, hops):
    up, down = shift_pairs(sections, dps, hops), shift_pairs(sections, dps, -hops)
    return [up[i] if i // dps % 2 == 0 else down[i] for i in range(sections * dps)]


def half_groups(sections):
    return [[s for s in range(sections) if s // 2 % 2 == half] for half in range(2)]


def plan_kernel(mine_ref, live_ref, order_ref, patches_ref, rows_ref, pick_far_ref, pick_near_ref):
    sections = live_ref.shape[1]
    keep = pick_far_ref.shape[0]
    mine = mine_ref[0]
    my_half = mine // 2 % 2
    live = live_ref[...].astype(jnp.float32)
    order = order_ref[...]
    down = lax.broadcasted_iota(jnp.int32, (sections, sections), 0)
    along = lax.broadcasted_iota(jnp.int32, (sections, sections), 1)
    live_down = jnp.sum(jnp.where(down == along, live, 0.0), axis=1, keepdims=True)
    starts_down = jnp.sum(jnp.where(along < down, live, 0.0), axis=1, keepdims=True)
    is_me = lax.broadcasted_iota(jnp.int32, (sections, 1), 0) == mine
    my_start = jnp.sum(jnp.where(is_me, starts_down, 0.0), axis=0, keepdims=True)
    my_live = jnp.sum(jnp.where(is_me, live_down, 0.0), axis=0, keepdims=True)
    peer = down // 2
    toward = jnp.where(down % 2 == 0, 1 - my_half, my_half)
    target = peer // 2 * 4 + toward * 2 + peer % 2
    place = jnp.sum(jnp.where(order == target, along, 0).astype(jnp.float32), axis=1, keepdims=True)
    slot = (place - my_start).astype(jnp.int32) & (sections - 1)
    wanted = (along == slot) & (slot.astype(jnp.float32) < my_live)
    move = jnp.where(wanted, 1.0, 0.0).astype(jnp.bfloat16)
    rows_ref[...] = jnp.dot(
        move, patches_ref[...], preferred_element_type=jnp.float32
    ).astype(jnp.bfloat16)
    lane = lax.broadcasted_iota(jnp.int32, (sections, sections), 1)
    source = lane // 4 * 4 + my_half * 2 + lane // 2 % 2
    from_it = down == source
    first = jnp.sum(jnp.where(from_it, starts_down, 0.0), axis=0, keepdims=True)
    last = first + jnp.sum(jnp.where(from_it, live_down, 0.0), axis=0, keepdims=True)
    rounds = lax.broadcasted_iota(jnp.int32, (keep, sections), 0) * sections
    lanes = lax.broadcasted_iota(jnp.int32, (1, sections), 1)
    for parity, owner, pick_ref in ((0, mine ^ 2, pick_far_ref), (1, mine, pick_near_ref)):
        at = jnp.sum(jnp.where(order == owner, lanes, 0).astype(jnp.float32), axis=1, keepdims=True)
        number = rounds.astype(jnp.float32) + at
        held = (number >= first) & (number < last) & (lanes % 2 == parity)
        pick_ref[...] = jnp.where(held, 1.0, 0.0).astype(jnp.bfloat16)


def plan(patches, live, order, mine, keep):
    slots, width = patches.shape
    vmem = pl.BlockSpec(memory_space=pltpu.VMEM)
    return pl.pallas_call(
        plan_kernel,
        out_shape=(
            jax.ShapeDtypeStruct((slots, width), jnp.bfloat16),
            jax.ShapeDtypeStruct((keep, slots), jnp.bfloat16),
            jax.ShapeDtypeStruct((keep, slots), jnp.bfloat16),
        ),
        in_specs=[pl.BlockSpec(memory_space=pltpu.SMEM), vmem, vmem, vmem],
        out_specs=(vmem, vmem, vmem),
        compiler_params=pltpu.CompilerParams(vmem_limit_bytes=16 * 1024 * 1024),
    )(mine[None], live, order, patches)


def away_kernel(rows_ref, part_ref, bias_ref, fetched_ref, out_ref, w1, w2, hidden, sems):
    units, width = w1.shape
    first = pltpu.make_async_copy(fetched_ref.at[pl.ds(0, units)], w1, sems.at[0])
    second = pltpu.make_async_copy(fetched_ref.at[pl.ds(units, units)], w2, sems.at[1])
    first.start()
    second.start()
    first.wait()
    for at in range(0, units, 256):
        span = pl.ds(at, min(256, units - at))
        pre = lax.dot_general(
            rows_ref[...], w1[span], (((1,), (1,)), ((), ())), preferred_element_type=jnp.float32
        ) + bias_ref[:, span]
        hidden[:, span] = (0.5 * pre * (1.0 + lax.erf(pre * np.float32(0.5**0.5)))).astype(jnp.bfloat16)
    second.wait()
    for at in range(0, width, 640):
        span = pl.ds(at, min(640, width - at))
        out = jnp.dot(hidden[...], w2[:, span], preferred_element_type=jnp.float32)
        out_ref[:, span] = (part_ref[:, span] + out).astype(jnp.bfloat16)


def add_away(rows, part, bias, fetched):
    count, width = rows.shape
    units = bias.shape[0]
    vmem = pl.BlockSpec(memory_space=pltpu.VMEM)
    return pl.pallas_call(
        away_kernel,
        out_shape=jax.ShapeDtypeStruct((count, width), jnp.bfloat16),
        in_specs=[vmem, vmem, vmem, pl.BlockSpec(memory_space=pl.ANY)],
        out_specs=vmem,
        scratch_shapes=[
            pltpu.VMEM((units, width), jnp.bfloat16),
            pltpu.VMEM((units, width), jnp.bfloat16),
            pltpu.VMEM((count, units), jnp.bfloat16),
            pltpu.SemaphoreType.DMA((2,)),
        ],
        compiler_params=pltpu.CompilerParams(vmem_limit_bytes=53 * 1024 * 1024),
    )(rows, part, bias[None], fetched)


def pick(chosen, rows):
    return jnp.dot(chosen, rows, preferred_element_type=jnp.float32).astype(jnp.bfloat16)


def per_device(
    patches, live, rounds, ln_gain, fc1_weight, fc1_bias, fc2_weight, fc2_bias, layer_scale
):
    sections = lax.axis_size("section")
    dps = lax.axis_size("dp")
    mine = lax.axis_index("section").astype(jnp.int32)
    keep = 3 * sections // 8
    groups = half_groups(sections)
    width, units = fc1_weight.shape
    f32 = jnp.float32

    def send(value, hops):
        return lax.ppermute(value, AXES, shift_pairs(sections, dps, hops))

    pieces = sections // 4
    depth = units // pieces
    member = (mine >> 2) * 2 + (mine & 1)
    first = (member & (pieces - 1)) * depth
    upper = member < pieces
    chosen = first + lax.broadcasted_iota(jnp.int32, (depth, units), 0)
    chosen = (chosen == lax.broadcasted_iota(jnp.int32, (depth, units), 1)).astype(jnp.bfloat16)
    piece1 = lax.dot_general(
        chosen, fc1_weight, (((1,), (1,)), ((), ())), preferred_element_type=f32
    ).astype(jnp.bfloat16)
    piece2 = lax.dynamic_slice_in_dim(fc2_weight, first, depth, axis=0)
    piece = jnp.where(upper, piece1, piece2)
    rows, pick_far, pick_near = plan(patches[0], live, rounds, mine, keep)
    away_bias = send(fc1_bias, dps // 2)
    away_bias, rows = lax.optimization_barrier((away_bias, rows))
    piece = lax.ppermute(piece, AXES, opposite_pairs(sections, dps, dps // 2))
    rows = lax.all_to_all(
        rows, "section", split_axis=0, concat_axis=0, axis_index_groups=groups, tiled=True
    )
    piece = lax.optimization_barrier((piece, rows))[0]
    fetched = lax.all_gather(piece, "section", axis=0, axis_index_groups=groups, tiled=True)
    crossing = pick(pick_far, rows)
    routed = pick(pick_near, rows) + send(crossing, dps)

    rows32 = routed.astype(f32)
    mean = jnp.mean(rows32, axis=1, keepdims=True)
    centered = rows32 - mean
    var = jnp.mean(centered * centered, axis=1, keepdims=True)
    normed = (centered * lax.rsqrt(var + 1e-06) * ln_gain).astype(jnp.bfloat16)

    up2, down2 = send(normed, 2), send(normed, -2)
    up13 = send(jnp.concatenate([normed, up2], axis=0), 1)
    down13 = send(jnp.concatenate([normed, down2], axis=0), -1)
    up4 = send(up2, 2)
    blocks = jnp.concatenate([up13, up2, up4, down13, down2, normed], axis=0)

    pre = jnp.dot(blocks, fc1_weight, preferred_element_type=f32) + fc1_bias
    hidden = jax.nn.gelu(pre, approximate=False).astype(jnp.bfloat16)
    part = jnp.dot(hidden, fc2_weight, preferred_element_type=f32)
    part = add_away(blocks, part, away_bias, fetched)

    def add(*parts):
        return sum(p.astype(f32) for p in parts)

    up02 = send(part[: 2 * keep], -1)
    up_far = send(part[3 * keep : 4 * keep], -2)
    down02 = send(part[4 * keep : 6 * keep], 1)
    up_sum = add(part[2 * keep : 3 * keep], up02[keep:], up_far).astype(jnp.bfloat16)
    down_sum = add(part[6 * keep : 7 * keep], down02[keep:]).astype(jnp.bfloat16)
    summed = add(send(up_sum, -2), up02[:keep], send(down_sum, 2), down02[:keep], part[7 * keep :])
    encoded = (rows32 + layer_scale * (summed + fc2_bias)).astype(jnp.bfloat16)
    return encoded[None]


def solution(mesh):
    placed = (
        P("dp", "section", None),
        P("dp", None),
        P("dp", None),
        P(),
        P(None, "dp"),
        P("dp"),
        P("dp", None),
        P(),
        P(),
    )
    return jax.shard_map(
        per_device, mesh=mesh, in_specs=placed, out_specs=P("dp", "section", None), check_vma=False
    )
```

```python
import jax
import jax.numpy as jnp
import numpy as np
from jax import lax
from jax.experimental import pallas as pl
from jax.experimental.pallas import tpu as pltpu
from jax.sharding import PartitionSpec as P

AXES = ("section", "dp")


def shift_pairs(sections, dps, hops):
    ring = 2 * dps
    pairs = []
    for section in range(sections):
        for dp in range(dps):
            there = (section // 2 % 2 * dps + dp + hops) % ring
            target = (section // 4 * 2 + there // dps) * 2 + section % 2
            pairs.append((section * dps + dp, target * dps + there % dps))
    return pairs


def opposite_pairs(sections, dps, hops):
    up, down = shift_pairs(sections, dps, hops), shift_pairs(sections, dps, -hops)
    return [up[i] if i // dps % 2 == 0 else down[i] for i in range(sections * dps)]


def half_groups(sections):
    return [[s for s in range(sections) if s // 2 % 2 == half] for half in range(2)]


def plan_kernel(mine_ref, live_ref, order_ref, patches_ref, rows_ref, pick_far_ref, pick_near_ref):
    sections = live_ref.shape[1]
    keep = pick_far_ref.shape[0]
    mine = mine_ref[0]
    my_half = mine // 2 % 2
    live = live_ref[...].astype(jnp.float32)
    order = order_ref[...]
    down = lax.broadcasted_iota(jnp.int32, (sections, sections), 0)
    along = lax.broadcasted_iota(jnp.int32, (sections, sections), 1)
    live_down = jnp.sum(jnp.where(down == along, live, 0.0), axis=1, keepdims=True)
    starts_down = jnp.sum(jnp.where(along < down, live, 0.0), axis=1, keepdims=True)
    is_me = lax.broadcasted_iota(jnp.int32, (sections, 1), 0) == mine
    my_start = jnp.sum(jnp.where(is_me, starts_down, 0.0), axis=0, keepdims=True)
    my_live = jnp.sum(jnp.where(is_me, live_down, 0.0), axis=0, keepdims=True)
    peer = down // 2
    toward = jnp.where(down % 2 == 0, 1 - my_half, my_half)
    target = peer // 2 * 4 + toward * 2 + peer % 2
    place = jnp.sum(jnp.where(order == target, along, 0).astype(jnp.float32), axis=1, keepdims=True)
    slot = (place - my_start).astype(jnp.int32) & (sections - 1)
    wanted = (along == slot) & (slot.astype(jnp.float32) < my_live)
    move = jnp.where(wanted, 1.0, 0.0).astype(jnp.bfloat16)
    rows_ref[...] = jnp.dot(
        move, patches_ref[...], preferred_element_type=jnp.float32
    ).astype(jnp.bfloat16)
    lane = lax.broadcasted_iota(jnp.int32, (sections, sections), 1)
    source = lane // 4 * 4 + my_half * 2 + lane // 2 % 2
    from_it = down == source
    first = jnp.sum(jnp.where(from_it, starts_down, 0.0), axis=0, keepdims=True)
    last = first + jnp.sum(jnp.where(from_it, live_down, 0.0), axis=0, keepdims=True)
    rounds = lax.broadcasted_iota(jnp.int32, (keep, sections), 0) * sections
    lanes = lax.broadcasted_iota(jnp.int32, (1, sections), 1)
    for parity, owner, pick_ref in ((0, mine ^ 2, pick_far_ref), (1, mine, pick_near_ref)):
        at = jnp.sum(jnp.where(order == owner, lanes, 0).astype(jnp.float32), axis=1, keepdims=True)
        number = rounds.astype(jnp.float32) + at
        held = (number >= first) & (number < last) & (lanes % 2 == parity)
        pick_ref[...] = jnp.where(held, 1.0, 0.0).astype(jnp.bfloat16)


def plan(patches, live, order, mine, keep):
    slots, width = patches.shape
    vmem = pl.BlockSpec(memory_space=pltpu.VMEM)
    return pl.pallas_call(
        plan_kernel,
        out_shape=(
            jax.ShapeDtypeStruct((slots, width), jnp.bfloat16),
            jax.ShapeDtypeStruct((keep, slots), jnp.bfloat16),
            jax.ShapeDtypeStruct((keep, slots), jnp.bfloat16),
        ),
        in_specs=[pl.BlockSpec(memory_space=pltpu.SMEM), vmem, vmem, vmem],
        out_specs=(vmem, vmem, vmem),
        compiler_params=pltpu.CompilerParams(vmem_limit_bytes=16 * 1024 * 1024),
    )(mine[None], live, order, patches)


def away_kernel(rows_ref, part_ref, bias_ref, fetched_ref, out_ref, hidden):
    width = rows_ref.shape[1]
    units = hidden.shape[1]
    for at in range(0, units, 256):
        size = min(256, units - at)
        span = pl.ds(at, size)
        pre = lax.dot_general(
            rows_ref[...], fetched_ref[span], (((1,), (1,)), ((), ())), preferred_element_type=jnp.float32
        ) + bias_ref[:, span]
        hidden[:, span] = (0.5 * pre * (1.0 + lax.erf(pre * np.float32(0.5**0.5)))).astype(jnp.bfloat16)
    for at in range(0, width, 640):
        span = pl.ds(at, min(640, width - at))
        out = jnp.dot(hidden[...], fetched_ref[pl.ds(units, units), span], preferred_element_type=jnp.float32)
        out_ref[:, span] = (part_ref[:, span] + out).astype(jnp.bfloat16)


def add_away(rows, part, bias, fetched):
    count, width = rows.shape
    units = bias.shape[0]
    vmem = pl.BlockSpec(memory_space=pltpu.VMEM)
    return pl.pallas_call(
        away_kernel,
        out_shape=jax.ShapeDtypeStruct((count, width), jnp.bfloat16),
        in_specs=[vmem, vmem, vmem, vmem],
        out_specs=vmem,
        scratch_shapes=[
            pltpu.VMEM((count, units), jnp.bfloat16),
        ],
        compiler_params=pltpu.CompilerParams(vmem_limit_bytes=28 * 1024 * 1024),
    )(rows, part, bias[None], fetched)


def pick(chosen, rows):
    return jnp.dot(chosen, rows, preferred_element_type=jnp.float32).astype(jnp.bfloat16)


def per_device(
    patches, live, rounds, ln_gain, fc1_weight, fc1_bias, fc2_weight, fc2_bias, layer_scale
):
    sections = lax.axis_size("section")
    dps = lax.axis_size("dp")
    mine = lax.axis_index("section").astype(jnp.int32)
    keep = 3 * sections // 8
    groups = half_groups(sections)
    width, units = fc1_weight.shape
    f32 = jnp.float32

    def send(value, hops):
        return lax.ppermute(value, AXES, shift_pairs(sections, dps, hops))

    pieces = sections // 4
    depth = units // pieces
    member = (mine >> 2) * 2 + (mine & 1)
    first = (member & (pieces - 1)) * depth
    upper = member < pieces
    chosen = first + lax.broadcasted_iota(jnp.int32, (depth, units), 0)
    chosen = (chosen == lax.broadcasted_iota(jnp.int32, (depth, units), 1)).astype(jnp.bfloat16)
    piece1 = lax.dot_general(
        chosen, fc1_weight, (((1,), (1,)), ((), ())), preferred_element_type=f32
    ).astype(jnp.bfloat16)
    piece2 = lax.dynamic_slice_in_dim(fc2_weight, first, depth, axis=0)
    piece = jnp.where(upper, piece1, piece2)
    piece, live = lax.optimization_barrier((piece, live))
    rows, pick_far, pick_near = plan(patches[0], live, rounds, mine, keep)
    piece = lax.ppermute(piece, AXES, opposite_pairs(sections, dps, dps // 2))
    rows = lax.all_to_all(
        rows, "section", split_axis=0, concat_axis=0, axis_index_groups=groups, tiled=True
    )
    piece = lax.optimization_barrier((piece, rows))[0]
    fetched = lax.all_gather(piece, "section", axis=0, axis_index_groups=groups, tiled=True)
    crossing = pick(pick_far, rows)
    bias = lax.optimization_barrier((fc1_bias, crossing))[0]
    away_bias = send(bias, dps // 2)
    crossed, away_bias = lax.optimization_barrier((send(crossing, dps), away_bias))
    routed = pick(pick_near, rows) + crossed

    rows32 = routed.astype(f32)
    mean = jnp.mean(rows32, axis=1, keepdims=True)
    centered = rows32 - mean
    var = jnp.mean(centered * centered, axis=1, keepdims=True)
    normed = (centered * lax.rsqrt(var + 1e-06) * ln_gain).astype(jnp.bfloat16)

    up2, down2 = send(normed, 2), send(normed, -2)
    up13 = send(jnp.concatenate([normed, up2], axis=0), 1)
    down13 = send(jnp.concatenate([normed, down2], axis=0), -1)
    up4 = send(up2, 2)
    blocks = jnp.concatenate([up13, up2, up4, down13, down2, normed], axis=0)

    pre = jnp.dot(blocks, fc1_weight, preferred_element_type=f32) + fc1_bias
    hidden = jax.nn.gelu(pre, approximate=False).astype(jnp.bfloat16)
    part = jnp.dot(hidden, fc2_weight, preferred_element_type=f32)
    part = add_away(blocks, part, away_bias, fetched)

    def add(*parts):
        return sum(p.astype(f32) for p in parts)

    up02 = send(part[: 2 * keep], -1)
    up_far = send(part[3 * keep : 4 * keep], -2)
    down02 = send(part[4 * keep : 6 * keep], 1)
    up_sum = add(part[2 * keep : 3 * keep], up02[keep:], up_far).astype(jnp.bfloat16)
    down_sum = add(part[6 * keep : 7 * keep], down02[keep:]).astype(jnp.bfloat16)
    summed = add(send(up_sum, -2), up02[:keep], send(down_sum, 2), down02[:keep], part[7 * keep :])
    encoded = (rows32 + layer_scale * (summed + fc2_bias)).astype(jnp.bfloat16)
    return encoded[None]


def solution(mesh):
    placed = (
        P("dp", "section", None),
        P("dp", None),
        P("dp", None),
        P(),
        P(None, "dp"),
        P("dp"),
        P("dp", None),
        P(),
        P(),
    )
    return jax.shard_map(
        per_device, mesh=mesh, in_specs=placed, out_specs=P("dp", "section", None), check_vma=False
    )
```

```python
import jax
import jax.numpy as jnp
import numpy as np
from jax import lax
from jax.experimental import pallas as pl
from jax.experimental.pallas import tpu as pltpu
from jax.sharding import PartitionSpec as P

AXES = ("section", "dp")


def shift_pairs(sections, dps, hops):
    ring = 2 * dps
    pairs = []
    for section in range(sections):
        for dp in range(dps):
            there = (section // 2 % 2 * dps + dp + hops) % ring
            target = (section // 4 * 2 + there // dps) * 2 + section % 2
            pairs.append((section * dps + dp, target * dps + there % dps))
    return pairs


def opposite_pairs(sections, dps, hops):
    up, down = shift_pairs(sections, dps, hops), shift_pairs(sections, dps, -hops)
    return [up[i] if i // dps % 2 == 0 else down[i] for i in range(sections * dps)]


def half_groups(sections):
    return [[s for s in range(sections) if s // 2 % 2 == half] for half in range(2)]


def plan_kernel(mine_ref, live_ref, order_ref, patches_ref, rows_ref, pick_far_ref, pick_near_ref):
    sections = live_ref.shape[1]
    keep = pick_far_ref.shape[0]
    mine = mine_ref[0]
    my_half = mine // 2 % 2
    live = live_ref[...].astype(jnp.float32)
    order = order_ref[...]
    down = lax.broadcasted_iota(jnp.int32, (sections, sections), 0)
    along = lax.broadcasted_iota(jnp.int32, (sections, sections), 1)
    live_down = jnp.sum(jnp.where(down == along, live, 0.0), axis=1, keepdims=True)
    starts_down = jnp.sum(jnp.where(along < down, live, 0.0), axis=1, keepdims=True)
    is_me = lax.broadcasted_iota(jnp.int32, (sections, 1), 0) == mine
    my_start = jnp.sum(jnp.where(is_me, starts_down, 0.0), axis=0, keepdims=True)
    my_live = jnp.sum(jnp.where(is_me, live_down, 0.0), axis=0, keepdims=True)
    peer = down // 2
    toward = jnp.where(down % 2 == 0, 1 - my_half, my_half)
    target = peer // 2 * 4 + toward * 2 + peer % 2
    place = jnp.sum(jnp.where(order == target, along, 0).astype(jnp.float32), axis=1, keepdims=True)
    slot = (place - my_start).astype(jnp.int32) & (sections - 1)
    wanted = (along == slot) & (slot.astype(jnp.float32) < my_live)
    move = jnp.where(wanted, 1.0, 0.0).astype(jnp.bfloat16)
    rows_ref[...] = jnp.dot(
        move, patches_ref[...], preferred_element_type=jnp.float32
    ).astype(jnp.bfloat16)
    lane = lax.broadcasted_iota(jnp.int32, (sections, sections), 1)
    source = lane // 4 * 4 + my_half * 2 + lane // 2 % 2
    from_it = down == source
    first = jnp.sum(jnp.where(from_it, starts_down, 0.0), axis=0, keepdims=True)
    last = first + jnp.sum(jnp.where(from_it, live_down, 0.0), axis=0, keepdims=True)
    rounds = lax.broadcasted_iota(jnp.int32, (keep, sections), 0) * sections
    lanes = lax.broadcasted_iota(jnp.int32, (1, sections), 1)
    for parity, owner, pick_ref in ((0, mine ^ 2, pick_far_ref), (1, mine, pick_near_ref)):
        at = jnp.sum(jnp.where(order == owner, lanes, 0).astype(jnp.float32), axis=1, keepdims=True)
        number = rounds.astype(jnp.float32) + at
        held = (number >= first) & (number < last) & (lanes % 2 == parity)
        pick_ref[...] = jnp.where(held, 1.0, 0.0).astype(jnp.bfloat16)


def plan(patches, live, order, mine, keep):
    slots, width = patches.shape
    vmem = pl.BlockSpec(memory_space=pltpu.VMEM)
    return pl.pallas_call(
        plan_kernel,
        out_shape=(
            jax.ShapeDtypeStruct((slots, width), jnp.bfloat16),
            jax.ShapeDtypeStruct((keep, slots), jnp.bfloat16),
            jax.ShapeDtypeStruct((keep, slots), jnp.bfloat16),
        ),
        in_specs=[pl.BlockSpec(memory_space=pltpu.SMEM), vmem, vmem, vmem],
        out_specs=(vmem, vmem, vmem),
        compiler_params=pltpu.CompilerParams(vmem_limit_bytes=16 * 1024 * 1024),
    )(mine[None], live, order, patches)


def away_kernel(rows_ref, part_ref, bias_ref, fetched_ref, out_ref, w1, w2, hidden, sems):
    units, width = w1.shape
    first = pltpu.make_async_copy(fetched_ref.at[pl.ds(0, units)], w1, sems.at[0])
    second = pltpu.make_async_copy(fetched_ref.at[pl.ds(units, units)], w2, sems.at[1])
    first.start()
    second.start()
    first.wait()
    for at in range(0, units, 256):
        span = pl.ds(at, min(256, units - at))
        pre = lax.dot_general(
            rows_ref[...], w1[span], (((1,), (1,)), ((), ())), preferred_element_type=jnp.float32
        ) + bias_ref[:, span]
        hidden[:, span] = (0.5 * pre * (1.0 + lax.erf(pre * np.float32(0.5**0.5)))).astype(jnp.bfloat16)
    second.wait()
    for at in range(0, width, 640):
        span = pl.ds(at, min(640, width - at))
        out = jnp.dot(hidden[...], w2[:, span], preferred_element_type=jnp.float32)
        out_ref[:, span] = (part_ref[:, span] + out).astype(jnp.bfloat16)


def add_away(rows, part, bias, fetched):
    count, width = rows.shape
    units = bias.shape[0]
    vmem = pl.BlockSpec(memory_space=pltpu.VMEM)
    return pl.pallas_call(
        away_kernel,
        out_shape=jax.ShapeDtypeStruct((count, width), jnp.bfloat16),
        in_specs=[vmem, vmem, vmem, pl.BlockSpec(memory_space=pl.ANY)],
        out_specs=vmem,
        scratch_shapes=[
            pltpu.VMEM((units, width), jnp.bfloat16),
            pltpu.VMEM((units, width), jnp.bfloat16),
            pltpu.VMEM((count, units), jnp.bfloat16),
            pltpu.SemaphoreType.DMA((2,)),
        ],
        compiler_params=pltpu.CompilerParams(vmem_limit_bytes=46 * 1024 * 1024),
    )(rows, part, bias[None], fetched)


def pick(chosen, rows):
    return jnp.dot(chosen, rows, preferred_element_type=jnp.float32).astype(jnp.bfloat16)


def per_device(
    patches, live, rounds, ln_gain, fc1_weight, fc1_bias, fc2_weight, fc2_bias, layer_scale
):
    sections = lax.axis_size("section")
    dps = lax.axis_size("dp")
    mine = lax.axis_index("section").astype(jnp.int32)
    keep = 3 * sections // 8
    groups = half_groups(sections)
    width, units = fc1_weight.shape
    f32 = jnp.float32

    def send(value, hops):
        return lax.ppermute(value, AXES, shift_pairs(sections, dps, hops))

    pieces = sections // 4
    depth = units // pieces
    member = (mine >> 2) * 2 + (mine & 1)
    first = (member & (pieces - 1)) * depth
    upper = member < pieces
    chosen = first + lax.broadcasted_iota(jnp.int32, (depth, units), 0)
    chosen = (chosen == lax.broadcasted_iota(jnp.int32, (depth, units), 1)).astype(jnp.bfloat16)
    piece1 = lax.dot_general(
        chosen, fc1_weight, (((1,), (1,)), ((), ())), preferred_element_type=f32
    ).astype(jnp.bfloat16)
    piece2 = lax.dynamic_slice_in_dim(fc2_weight, first, depth, axis=0)
    piece = jnp.where(upper, piece1, piece2)
    piece, live = lax.optimization_barrier((piece, live))
    rows, pick_far, pick_near = plan(patches[0], live, rounds, mine, keep)
    piece = lax.ppermute(piece, AXES, opposite_pairs(sections, dps, dps // 2))
    rows = lax.all_to_all(
        rows, "section", split_axis=0, concat_axis=0, axis_index_groups=groups, tiled=True
    )
    rows = lax.optimization_barrier((rows, piece))[0]
    fetched = lax.all_gather(piece, "section", axis=0, axis_index_groups=groups, tiled=True)
    crossing = pick(pick_far, rows)
    bias = lax.optimization_barrier((fc1_bias, crossing))[0]
    away_bias = send(bias, dps // 2)
    crossed, away_bias = lax.optimization_barrier((send(crossing, dps), away_bias))
    routed = pick(pick_near, rows) + crossed

    rows32 = routed.astype(f32)
    mean = jnp.mean(rows32, axis=1, keepdims=True)
    centered = rows32 - mean
    var = jnp.mean(centered * centered, axis=1, keepdims=True)
    normed = (centered * lax.rsqrt(var + 1e-06) * ln_gain).astype(jnp.bfloat16)

    up2, down2 = send(normed, 2), send(normed, -2)
    up13 = send(jnp.concatenate([normed, up2], axis=0), 1)
    down13 = send(jnp.concatenate([normed, down2], axis=0), -1)
    up4 = send(up2, 2)
    blocks = jnp.concatenate([up13, up2, up4, down13, down2, normed], axis=0)

    pre = jnp.dot(blocks, fc1_weight, preferred_element_type=f32) + fc1_bias
    hidden = jax.nn.gelu(pre, approximate=False).astype(jnp.bfloat16)
    part = jnp.dot(hidden, fc2_weight, preferred_element_type=f32)
    part = add_away(blocks, part, away_bias, fetched)

    def add(*parts):
        return sum(p.astype(f32) for p in parts)

    up02 = send(part[: 2 * keep], -1)
    up_far = send(part[3 * keep : 4 * keep], -2)
    down02 = send(part[4 * keep : 6 * keep], 1)
    up_sum = add(part[2 * keep : 3 * keep], up02[keep:], up_far).astype(jnp.bfloat16)
    down_sum = add(part[6 * keep : 7 * keep], down02[keep:]).astype(jnp.bfloat16)
    summed = add(send(up_sum, -2), up02[:keep], send(down_sum, 2), down02[:keep], part[7 * keep :])
    encoded = (rows32 + layer_scale * (summed + fc2_bias)).astype(jnp.bfloat16)
    return encoded[None]


def solution(mesh):
    placed = (
        P("dp", "section", None),
        P("dp", None),
        P("dp", None),
        P(),
        P(None, "dp"),
        P("dp"),
        P("dp", None),
        P(),
        P(),
    )
    return jax.shard_map(
        per_device, mesh=mesh, in_specs=placed, out_specs=P("dp", "section", None), check_vma=False
    )
```

```python
import jax
import jax.numpy as jnp
import numpy as np
from jax import lax
from jax.experimental import pallas as pl
from jax.experimental.pallas import tpu as pltpu
from jax.sharding import PartitionSpec as P

AXES = ("section", "dp")


def shift_pairs(sections, dps, hops):
    ring = 2 * dps
    pairs = []
    for section in range(sections):
        for dp in range(dps):
            there = (section // 2 % 2 * dps + dp + hops) % ring
            target = (section // 4 * 2 + there // dps) * 2 + section % 2
            pairs.append((section * dps + dp, target * dps + there % dps))
    return pairs


def opposite_pairs(sections, dps, hops):
    up, down = shift_pairs(sections, dps, hops), shift_pairs(sections, dps, -hops)
    return [up[i] if i // dps % 2 == 0 else down[i] for i in range(sections * dps)]


def half_groups(sections):
    return [[s for s in range(sections) if s // 2 % 2 == half] for half in range(2)]


def plan_kernel(mine_ref, live_ref, order_ref, patches_ref, rows_ref, pick_far_ref, pick_near_ref):
    sections = live_ref.shape[1]
    keep = pick_far_ref.shape[0]
    mine = mine_ref[0]
    my_half = mine // 2 % 2
    live = live_ref[...].astype(jnp.float32)
    order = order_ref[...]
    down = lax.broadcasted_iota(jnp.int32, (sections, sections), 0)
    along = lax.broadcasted_iota(jnp.int32, (sections, sections), 1)
    live_down = jnp.sum(jnp.where(down == along, live, 0.0), axis=1, keepdims=True)
    starts_down = jnp.sum(jnp.where(along < down, live, 0.0), axis=1, keepdims=True)
    is_me = lax.broadcasted_iota(jnp.int32, (sections, 1), 0) == mine
    my_start = jnp.sum(jnp.where(is_me, starts_down, 0.0), axis=0, keepdims=True)
    my_live = jnp.sum(jnp.where(is_me, live_down, 0.0), axis=0, keepdims=True)
    peer = down // 2
    toward = jnp.where(down % 2 == 0, 1 - my_half, my_half)
    target = peer // 2 * 4 + toward * 2 + peer % 2
    place = jnp.sum(jnp.where(order == target, along, 0).astype(jnp.float32), axis=1, keepdims=True)
    slot = (place - my_start).astype(jnp.int32) & (sections - 1)
    wanted = (along == slot) & (slot.astype(jnp.float32) < my_live)
    move = jnp.where(wanted, 1.0, 0.0).astype(jnp.bfloat16)
    rows_ref[...] = jnp.dot(
        move, patches_ref[...], preferred_element_type=jnp.float32
    ).astype(jnp.bfloat16)
    lane = lax.broadcasted_iota(jnp.int32, (sections, sections), 1)
    source = lane // 4 * 4 + my_half * 2 + lane // 2 % 2
    from_it = down == source
    first = jnp.sum(jnp.where(from_it, starts_down, 0.0), axis=0, keepdims=True)
    last = first + jnp.sum(jnp.where(from_it, live_down, 0.0), axis=0, keepdims=True)
    rounds = lax.broadcasted_iota(jnp.int32, (keep, sections), 0) * sections
    lanes = lax.broadcasted_iota(jnp.int32, (1, sections), 1)
    for parity, owner, pick_ref in ((0, mine ^ 2, pick_far_ref), (1, mine, pick_near_ref)):
        at = jnp.sum(jnp.where(order == owner, lanes, 0).astype(jnp.float32), axis=1, keepdims=True)
        number = rounds.astype(jnp.float32) + at
        held = (number >= first) & (number < last) & (lanes % 2 == parity)
        pick_ref[...] = jnp.where(held, 1.0, 0.0).astype(jnp.bfloat16)


def plan(patches, live, order, mine, keep):
    slots, width = patches.shape
    vmem = pl.BlockSpec(memory_space=pltpu.VMEM)
    return pl.pallas_call(
        plan_kernel,
        out_shape=(
            jax.ShapeDtypeStruct((slots, width), jnp.bfloat16),
            jax.ShapeDtypeStruct((keep, slots), jnp.bfloat16),
            jax.ShapeDtypeStruct((keep, slots), jnp.bfloat16),
        ),
        in_specs=[pl.BlockSpec(memory_space=pltpu.SMEM), vmem, vmem, vmem],
        out_specs=(vmem, vmem, vmem),
        compiler_params=pltpu.CompilerParams(vmem_limit_bytes=16 * 1024 * 1024),
    )(mine[None], live, order, patches)


def away_kernel(rows_ref, part_ref, bias_ref, fetched_ref, out_ref, w1, w2, hidden, sems):
    units, width = w1.shape
    first = pltpu.make_async_copy(fetched_ref.at[pl.ds(0, units)], w1, sems.at[0])
    second = pltpu.make_async_copy(fetched_ref.at[pl.ds(units, units)], w2, sems.at[1])
    first.start()
    second.start()
    first.wait()
    for at in range(0, units, 256):
        span = pl.ds(at, min(256, units - at))
        pre = lax.dot_general(
            rows_ref[...], w1[span], (((1,), (1,)), ((), ())), preferred_element_type=jnp.float32
        ) + bias_ref[:, span]
        hidden[:, span] = (0.5 * pre * (1.0 + lax.erf(pre * np.float32(0.5**0.5)))).astype(jnp.bfloat16)
    second.wait()
    for at in range(0, width, 640):
        span = pl.ds(at, min(640, width - at))
        out = jnp.dot(hidden[...], w2[:, span], preferred_element_type=jnp.float32)
        out_ref[:, span] = (part_ref[:, span] + out).astype(jnp.bfloat16)


def add_away(rows, part, bias, fetched):
    count, width = rows.shape
    units = bias.shape[0]
    vmem = pl.BlockSpec(memory_space=pltpu.VMEM)
    return pl.pallas_call(
        away_kernel,
        out_shape=jax.ShapeDtypeStruct((count, width), jnp.bfloat16),
        in_specs=[vmem, vmem, vmem, pl.BlockSpec(memory_space=pl.ANY)],
        out_specs=vmem,
        scratch_shapes=[
            pltpu.VMEM((units, width), jnp.bfloat16),
            pltpu.VMEM((units, width), jnp.bfloat16),
            pltpu.VMEM((count, units), jnp.bfloat16),
            pltpu.SemaphoreType.DMA((2,)),
        ],
        compiler_params=pltpu.CompilerParams(vmem_limit_bytes=46 * 1024 * 1024),
    )(rows, part, bias[None], fetched)


def pick(chosen, rows):
    return jnp.dot(chosen, rows, preferred_element_type=jnp.float32).astype(jnp.bfloat16)


def per_device(
    patches, live, rounds, ln_gain, fc1_weight, fc1_bias, fc2_weight, fc2_bias, layer_scale
):
    sections = lax.axis_size("section")
    dps = lax.axis_size("dp")
    mine = lax.axis_index("section").astype(jnp.int32)
    keep = 3 * sections // 8
    groups = half_groups(sections)
    width, units = fc1_weight.shape
    f32 = jnp.float32

    def send(value, hops):
        return lax.ppermute(value, AXES, shift_pairs(sections, dps, hops))

    pieces = sections // 4
    depth = units // pieces
    member = (mine >> 2) * 2 + (mine & 1)
    first = (member & (pieces - 1)) * depth
    upper = member < pieces
    chosen = first + lax.broadcasted_iota(jnp.int32, (depth, units), 0)
    chosen = (chosen == lax.broadcasted_iota(jnp.int32, (depth, units), 1)).astype(jnp.bfloat16)
    piece1 = lax.dot_general(
        chosen, fc1_weight, (((1,), (1,)), ((), ())), preferred_element_type=f32
    ).astype(jnp.bfloat16)
    piece2 = lax.dynamic_slice_in_dim(fc2_weight, first, depth, axis=0)
    piece = jnp.where(upper, piece1, piece2)
    piece, live = lax.optimization_barrier((piece, live))
    rows, pick_far, pick_near = plan(patches[0], live, rounds, mine, keep)
    piece = lax.ppermute(piece, AXES, opposite_pairs(sections, dps, dps // 2))
    rows = lax.cond(
        live[0, 0] > 0,
        lambda rows: lax.all_to_all(
            rows, "section", split_axis=0, concat_axis=0, axis_index_groups=groups, tiled=True
        ),
        jnp.zeros_like,
        rows,
    )
    piece = lax.optimization_barrier((piece, rows))[0]
    fetched = lax.all_gather(piece, "section", axis=0, axis_index_groups=groups, tiled=True)
    crossing = pick(pick_far, rows)
    bias = lax.optimization_barrier((fc1_bias, crossing))[0]
    away_bias = send(bias, dps // 2)
    crossed, away_bias = lax.optimization_barrier((send(crossing, dps), away_bias))
    routed = pick(pick_near, rows) + crossed

    rows32 = routed.astype(f32)
    mean = jnp.mean(rows32, axis=1, keepdims=True)
    centered = rows32 - mean
    var = jnp.mean(centered * centered, axis=1, keepdims=True)
    normed = (centered * lax.rsqrt(var + 1e-06) * ln_gain).astype(jnp.bfloat16)

    up2, down2 = send(normed, 2), send(normed, -2)
    up13 = send(jnp.concatenate([normed, up2], axis=0), 1)
    down13 = send(jnp.concatenate([normed, down2], axis=0), -1)
    up4 = send(up2, 2)
    blocks = jnp.concatenate([up13, up2, up4, down13, down2, normed], axis=0)

    pre = jnp.dot(blocks, fc1_weight, preferred_element_type=f32) + fc1_bias
    hidden = jax.nn.gelu(pre, approximate=False).astype(jnp.bfloat16)
    part = jnp.dot(hidden, fc2_weight, preferred_element_type=f32)
    part = add_away(blocks, part, away_bias, fetched)

    def add(*parts):
        return sum(p.astype(f32) for p in parts)

    up02 = send(part[: 2 * keep], -1)
    up_far = send(part[3 * keep : 4 * keep], -2)
    down02 = send(part[4 * keep : 6 * keep], 1)
    up_sum = add(part[2 * keep : 3 * keep], up02[keep:], up_far).astype(jnp.bfloat16)
    down_sum = add(part[6 * keep : 7 * keep], down02[keep:]).astype(jnp.bfloat16)
    summed = add(send(up_sum, -2), up02[:keep], send(down_sum, 2), down02[:keep], part[7 * keep :])
    encoded = (rows32 + layer_scale * (summed + fc2_bias)).astype(jnp.bfloat16)
    return encoded[None]


def solution(mesh):
    placed = (
        P("dp", "section", None),
        P("dp", None),
        P("dp", None),
        P(),
        P(None, "dp"),
        P("dp"),
        P("dp", None),
        P(),
        P(),
    )
    return jax.shard_map(
        per_device, mesh=mesh, in_specs=placed, out_specs=P("dp", "section", None), check_vma=False
    )
```

```python
import jax
import jax.numpy as jnp
import numpy as np
from jax import lax
from jax.experimental import pallas as pl
from jax.experimental.pallas import tpu as pltpu
from jax.sharding import PartitionSpec as P

AXES = ("section", "dp")


def shift_pairs(sections, dps, hops):
    ring = 2 * dps
    pairs = []
    for section in range(sections):
        for dp in range(dps):
            there = (section // 2 % 2 * dps + dp + hops) % ring
            target = (section // 4 * 2 + there // dps) * 2 + section % 2
            pairs.append((section * dps + dp, target * dps + there % dps))
    return pairs


def opposite_pairs(sections, dps, hops):
    up, down = shift_pairs(sections, dps, hops), shift_pairs(sections, dps, -hops)
    return [up[i] if i // dps % 2 == 0 else down[i] for i in range(sections * dps)]


def half_groups(sections):
    return [[s for s in range(sections) if s // 2 % 2 == half] for half in range(2)]


def plan_kernel(mine_ref, live_ref, order_ref, patches_ref, rows_ref, pick_far_ref, pick_near_ref):
    sections = live_ref.shape[1]
    keep = pick_far_ref.shape[0]
    mine = mine_ref[0]
    my_half = mine // 2 % 2
    live = live_ref[...].astype(jnp.float32)
    order = order_ref[...]
    down = lax.broadcasted_iota(jnp.int32, (sections, sections), 0)
    along = lax.broadcasted_iota(jnp.int32, (sections, sections), 1)
    live_down = jnp.sum(jnp.where(down == along, live, 0.0), axis=1, keepdims=True)
    starts_down = jnp.sum(jnp.where(along < down, live, 0.0), axis=1, keepdims=True)
    is_me = lax.broadcasted_iota(jnp.int32, (sections, 1), 0) == mine
    my_start = jnp.sum(jnp.where(is_me, starts_down, 0.0), axis=0, keepdims=True)
    my_live = jnp.sum(jnp.where(is_me, live_down, 0.0), axis=0, keepdims=True)
    peer = down // 2
    toward = jnp.where(down % 2 == 0, 1 - my_half, my_half)
    target = peer // 2 * 4 + toward * 2 + peer % 2
    place = jnp.sum(jnp.where(order == target, along, 0).astype(jnp.float32), axis=1, keepdims=True)
    slot = (place - my_start).astype(jnp.int32) & (sections - 1)
    wanted = (along == slot) & (slot.astype(jnp.float32) < my_live)
    move = jnp.where(wanted, 1.0, 0.0).astype(jnp.bfloat16)
    rows_ref[...] = jnp.dot(
        move, patches_ref[...], preferred_element_type=jnp.float32
    ).astype(jnp.bfloat16)
    lane = lax.broadcasted_iota(jnp.int32, (sections, sections), 1)
    source = lane // 4 * 4 + my_half * 2 + lane // 2 % 2
    from_it = down == source
    first = jnp.sum(jnp.where(from_it, starts_down, 0.0), axis=0, keepdims=True)
    last = first + jnp.sum(jnp.where(from_it, live_down, 0.0), axis=0, keepdims=True)
    rounds = lax.broadcasted_iota(jnp.int32, (keep, sections), 0) * sections
    lanes = lax.broadcasted_iota(jnp.int32, (1, sections), 1)
    for parity, owner, pick_ref in ((0, mine ^ 2, pick_far_ref), (1, mine, pick_near_ref)):
        at = jnp.sum(jnp.where(order == owner, lanes, 0).astype(jnp.float32), axis=1, keepdims=True)
        number = rounds.astype(jnp.float32) + at
        held = (number >= first) & (number < last) & (lanes % 2 == parity)
        pick_ref[...] = jnp.where(held, 1.0, 0.0).astype(jnp.bfloat16)


def plan(patches, live, order, mine, keep):
    slots, width = patches.shape
    vmem = pl.BlockSpec(memory_space=pltpu.VMEM)
    return pl.pallas_call(
        plan_kernel,
        out_shape=(
            jax.ShapeDtypeStruct((slots, width), jnp.bfloat16),
            jax.ShapeDtypeStruct((keep, slots), jnp.bfloat16),
            jax.ShapeDtypeStruct((keep, slots), jnp.bfloat16),
        ),
        in_specs=[pl.BlockSpec(memory_space=pltpu.SMEM), vmem, vmem, vmem],
        out_specs=(vmem, vmem, vmem),
        compiler_params=pltpu.CompilerParams(vmem_limit_bytes=16 * 1024 * 1024),
    )(mine[None], live, order, patches)


def piece_kernel(mine_ref, fc1_ref, fc2_ref, out_ref, window, rows, sem):
    depth = out_ref.shape[0]
    units = fc1_ref.shape[1]
    mine = mine_ref[0]
    member = (mine >> 2) * 2 + (mine & 1)
    pieces = units // depth
    first = (member & (pieces - 1)) * depth

    def cut(source, held, start):
        copy = pltpu.make_async_copy(source, held, sem)
        copy.start()
        copy.wait()
        shape = (depth, held.shape[1] if held is window else held.shape[0])
        unit = first - start + lax.broadcasted_iota(jnp.int32, shape, 0)
        chosen = unit == lax.broadcasted_iota(jnp.int32, shape, 1)
        return jnp.where(chosen, 1.0, 0.0).astype(jnp.bfloat16)

    @pl.when(member < pieces)
    def _():
        start = pl.multiple_of(jnp.minimum((first >> 7) << 7, units - window.shape[1]), 128)
        chosen = cut(fc1_ref.at[:, pl.ds(start, window.shape[1])], window, start)
        out_ref[...] = lax.dot_general(
            chosen, window[...], (((1,), (1,)), ((), ())), preferred_element_type=jnp.float32
        ).astype(jnp.bfloat16)

    @pl.when(member >= pieces)
    def _():
        start = pl.multiple_of(jnp.minimum((first >> 4) << 4, units - rows.shape[0]), 16)
        chosen = cut(fc2_ref.at[pl.ds(start, rows.shape[0])], rows, start)
        out_ref[...] = jnp.dot(
            chosen, rows[...], preferred_element_type=jnp.float32
        ).astype(jnp.bfloat16)


def cut_piece(mine, fc1_weight, fc2_weight, depth):
    units, width = fc2_weight.shape
    anywhere = pl.BlockSpec(memory_space=pl.ANY)
    return pl.pallas_call(
        piece_kernel,
        out_shape=jax.ShapeDtypeStruct((depth, width), jnp.bfloat16),
        in_specs=[pl.BlockSpec(memory_space=pltpu.SMEM), anywhere, anywhere],
        out_specs=pl.BlockSpec(memory_space=pltpu.VMEM),
        scratch_shapes=[
            pltpu.VMEM((width, 256), jnp.bfloat16),
            pltpu.VMEM((64, width), jnp.bfloat16),
            pltpu.SemaphoreType.DMA,
        ],
        compiler_params=pltpu.CompilerParams(vmem_limit_bytes=50 * 1024 * 1024),
    )(mine[None], fc1_weight, fc2_weight)


def away_kernel(rows_ref, part_ref, bias_ref, fetched_ref, out_ref, w1, w2, hidden, sems):
    units, width = w1.shape
    spans = [(at, min(256, units - at)) for at in range(0, units, 256)]
    copies = [
        pltpu.make_async_copy(fetched_ref.at[pl.ds(at, size)], w1.at[pl.ds(at, size)], sems.at[i])
        for i, (at, size) in enumerate(spans)
    ]
    second = pltpu.make_async_copy(fetched_ref.at[pl.ds(units, units)], w2, sems.at[len(spans)])
    for copy in copies + [second]:
        copy.start()
    for copy, (at, size) in zip(copies, spans):
        copy.wait()
        span = pl.ds(at, size)
        pre = lax.dot_general(
            rows_ref[...], w1[span], (((1,), (1,)), ((), ())), preferred_element_type=jnp.float32
        ) + bias_ref[:, span]
        hidden[:, span] = (0.5 * pre * (1.0 + lax.erf(pre * np.float32(0.5**0.5)))).astype(jnp.bfloat16)
    second.wait()
    for at in range(0, width, 640):
        span = pl.ds(at, min(640, width - at))
        out = jnp.dot(hidden[...], w2[:, span], preferred_element_type=jnp.float32)
        out_ref[:, span] = (part_ref[:, span] + out).astype(jnp.bfloat16)


def add_away(rows, part, bias, fetched):
    count, width = rows.shape
    units = bias.shape[0]
    vmem = pl.BlockSpec(memory_space=pltpu.VMEM)
    return pl.pallas_call(
        away_kernel,
        out_shape=jax.ShapeDtypeStruct((count, width), jnp.bfloat16),
        in_specs=[vmem, vmem, vmem, pl.BlockSpec(memory_space=pl.ANY)],
        out_specs=vmem,
        scratch_shapes=[
            pltpu.VMEM((units, width), jnp.bfloat16),
            pltpu.VMEM((units, width), jnp.bfloat16),
            pltpu.VMEM((count, units), jnp.bfloat16),
            pltpu.SemaphoreType.DMA((1 + -(-units // 256),)),
        ],
        compiler_params=pltpu.CompilerParams(vmem_limit_bytes=46 * 1024 * 1024),
    )(rows, part, bias[None], fetched)


def pick(chosen, rows):
    return jnp.dot(chosen, rows, preferred_element_type=jnp.float32).astype(jnp.bfloat16)


def per_device(
    patches, live, rounds, ln_gain, fc1_weight, fc1_bias, fc2_weight, fc2_bias, layer_scale
):
    sections = lax.axis_size("section")
    dps = lax.axis_size("dp")
    mine = lax.axis_index("section").astype(jnp.int32)
    keep = 3 * sections // 8
    groups = half_groups(sections)
    width, units = fc1_weight.shape
    f32 = jnp.float32

    def send(value, hops):
        return lax.ppermute(value, AXES, shift_pairs(sections, dps, hops))

    pieces = sections // 4
    depth = units // pieces
    piece = cut_piece(mine, fc1_weight, fc2_weight, depth)
    piece, live = lax.optimization_barrier((piece, live))
    rows, pick_far, pick_near = plan(patches[0], live, rounds, mine, keep)
    piece = lax.ppermute(piece, AXES, opposite_pairs(sections, dps, dps // 2))
    rows = lax.cond(
        live[0, 0] > 0,
        lambda rows: lax.all_to_all(
            rows, "section", split_axis=0, concat_axis=0, axis_index_groups=groups, tiled=True
        ),
        jnp.zeros_like,
        rows,
    )
    piece = lax.optimization_barrier((piece, rows))[0]
    fetched = lax.all_gather(piece, "section", axis=0, axis_index_groups=groups, tiled=True)
    crossing = pick(pick_far, rows)
    bias = lax.optimization_barrier((fc1_bias, crossing))[0]
    away_bias = send(bias, dps // 2)
    crossed, away_bias = lax.optimization_barrier((send(crossing, dps), away_bias))
    routed = pick(pick_near, rows) + crossed

    rows32 = routed.astype(f32)
    mean = jnp.mean(rows32, axis=1, keepdims=True)
    centered = rows32 - mean
    var = jnp.mean(centered * centered, axis=1, keepdims=True)
    normed = (centered * lax.rsqrt(var + 1e-06) * ln_gain).astype(jnp.bfloat16)

    up2, down2 = send(normed, 2), send(normed, -2)
    up13 = send(jnp.concatenate([normed, up2], axis=0), 1)
    down13 = send(jnp.concatenate([normed, down2], axis=0), -1)
    up4 = send(up2, 2)
    blocks = jnp.concatenate([up13, up2, up4, down13, down2, normed], axis=0)

    pre = jnp.dot(blocks, fc1_weight, preferred_element_type=f32) + fc1_bias
    hidden = jax.nn.gelu(pre, approximate=False).astype(jnp.bfloat16)
    part = jnp.dot(hidden, fc2_weight, preferred_element_type=f32)
    part = add_away(blocks, part, away_bias, fetched)

    def add(*parts):
        return sum(p.astype(f32) for p in parts)

    up02 = send(part[: 2 * keep], -1)
    up_far = send(part[3 * keep : 4 * keep], -2)
    down02 = send(part[4 * keep : 6 * keep], 1)
    up_sum = add(part[2 * keep : 3 * keep], up02[keep:], up_far).astype(jnp.bfloat16)
    down_sum = add(part[6 * keep : 7 * keep], down02[keep:]).astype(jnp.bfloat16)
    summed = add(send(up_sum, -2), up02[:keep], send(down_sum, 2), down02[:keep], part[7 * keep :])
    encoded = (rows32 + layer_scale * (summed + fc2_bias)).astype(jnp.bfloat16)
    return encoded[None]


def solution(mesh):
    placed = (
        P("dp", "section", None),
        P("dp", None),
        P("dp", None),
        P(),
        P(None, "dp"),
        P("dp"),
        P("dp", None),
        P(),
        P(),
    )
    return jax.shard_map(
        per_device, mesh=mesh, in_specs=placed, out_specs=P("dp", "section", None), check_vma=False
    )
```

```python
import jax
import jax.numpy as jnp
import numpy as np
from jax import lax
from jax.experimental import pallas as pl
from jax.experimental.pallas import tpu as pltpu
from jax.sharding import PartitionSpec as P

AXES = ("section", "dp")


def shift_pairs(sections, dps, hops):
    ring = 2 * dps
    pairs = []
    for section in range(sections):
        for dp in range(dps):
            there = (section // 2 % 2 * dps + dp + hops) % ring
            target = (section // 4 * 2 + there // dps) * 2 + section % 2
            pairs.append((section * dps + dp, target * dps + there % dps))
    return pairs


def opposite_pairs(sections, dps, hops):
    up, down = shift_pairs(sections, dps, hops), shift_pairs(sections, dps, -hops)
    return [up[i] if i // dps % 2 == 0 else down[i] for i in range(sections * dps)]


def half_groups(sections):
    return [[s for s in range(sections) if s // 2 % 2 == half] for half in range(2)]


def plan_kernel(mine_ref, live_ref, order_ref, patches_ref, rows_ref, pick_far_ref, pick_near_ref):
    sections = live_ref.shape[1]
    keep = pick_far_ref.shape[0]
    mine = mine_ref[0]
    my_half = mine // 2 % 2
    live = live_ref[...].astype(jnp.float32)
    order = order_ref[...]
    down = lax.broadcasted_iota(jnp.int32, (sections, sections), 0)
    along = lax.broadcasted_iota(jnp.int32, (sections, sections), 1)
    live_down = jnp.sum(jnp.where(down == along, live, 0.0), axis=1, keepdims=True)
    starts_down = jnp.sum(jnp.where(along < down, live, 0.0), axis=1, keepdims=True)
    is_me = lax.broadcasted_iota(jnp.int32, (sections, 1), 0) == mine
    my_start = jnp.sum(jnp.where(is_me, starts_down, 0.0), axis=0, keepdims=True)
    my_live = jnp.sum(jnp.where(is_me, live_down, 0.0), axis=0, keepdims=True)
    peer = down // 2
    toward = jnp.where(down % 2 == 0, 1 - my_half, my_half)
    target = peer // 2 * 4 + toward * 2 + peer % 2
    place = jnp.sum(jnp.where(order == target, along, 0).astype(jnp.float32), axis=1, keepdims=True)
    slot = (place - my_start).astype(jnp.int32) & (sections - 1)
    wanted = (along == slot) & (slot.astype(jnp.float32) < my_live)
    move = jnp.where(wanted, 1.0, 0.0).astype(jnp.bfloat16)
    rows_ref[...] = jnp.dot(
        move, patches_ref[...], preferred_element_type=jnp.float32
    ).astype(jnp.bfloat16)
    lane = lax.broadcasted_iota(jnp.int32, (sections, sections), 1)
    source = lane // 4 * 4 + my_half * 2 + lane // 2 % 2
    from_it = down == source
    first = jnp.sum(jnp.where(from_it, starts_down, 0.0), axis=0, keepdims=True)
    last = first + jnp.sum(jnp.where(from_it, live_down, 0.0), axis=0, keepdims=True)
    rounds = lax.broadcasted_iota(jnp.int32, (keep, sections), 0) * sections
    lanes = lax.broadcasted_iota(jnp.int32, (1, sections), 1)
    for parity, owner, pick_ref in ((0, mine ^ 2, pick_far_ref), (1, mine, pick_near_ref)):
        at = jnp.sum(jnp.where(order == owner, lanes, 0).astype(jnp.float32), axis=1, keepdims=True)
        number = rounds.astype(jnp.float32) + at
        held = (number >= first) & (number < last) & (lanes % 2 == parity)
        pick_ref[...] = jnp.where(held, 1.0, 0.0).astype(jnp.bfloat16)


def plan(patches, live, order, mine, keep):
    slots, width = patches.shape
    vmem = pl.BlockSpec(memory_space=pltpu.VMEM)
    return pl.pallas_call(
        plan_kernel,
        out_shape=(
            jax.ShapeDtypeStruct((slots, width), jnp.bfloat16),
            jax.ShapeDtypeStruct((keep, slots), jnp.bfloat16),
            jax.ShapeDtypeStruct((keep, slots), jnp.bfloat16),
        ),
        in_specs=[pl.BlockSpec(memory_space=pltpu.SMEM), vmem, vmem, vmem],
        out_specs=(vmem, vmem, vmem),
        compiler_params=pltpu.CompilerParams(vmem_limit_bytes=16 * 1024 * 1024),
    )(mine[None], live, order, patches)


def piece_kernel(mine_ref, fc1_ref, fc2_ref, out_ref, window, rows, sem):
    depth = out_ref.shape[0]
    units = fc1_ref.shape[1]
    mine = mine_ref[0]
    member = (mine >> 2) * 2 + (mine & 1)
    pieces = units // depth
    first = (member & (pieces - 1)) * depth

    def cut(source, held, start):
        copy = pltpu.make_async_copy(source, held, sem)
        copy.start()
        copy.wait()
        shape = (depth, held.shape[1] if held is window else held.shape[0])
        unit = first - start + lax.broadcasted_iota(jnp.int32, shape, 0)
        chosen = unit == lax.broadcasted_iota(jnp.int32, shape, 1)
        return jnp.where(chosen, 1.0, 0.0).astype(jnp.bfloat16)

    @pl.when(member < pieces)
    def _():
        start = pl.multiple_of(jnp.minimum((first >> 7) << 7, units - window.shape[1]), 128)
        chosen = cut(fc1_ref.at[:, pl.ds(start, window.shape[1])], window, start)
        out_ref[...] = lax.dot_general(
            chosen, window[...], (((1,), (1,)), ((), ())), preferred_element_type=jnp.float32
        ).astype(jnp.bfloat16)

    @pl.when(member >= pieces)
    def _():
        start = pl.multiple_of(jnp.minimum((first >> 4) << 4, units - rows.shape[0]), 16)
        chosen = cut(fc2_ref.at[pl.ds(start, rows.shape[0])], rows, start)
        out_ref[...] = jnp.dot(
            chosen, rows[...], preferred_element_type=jnp.float32
        ).astype(jnp.bfloat16)


def cut_piece(mine, fc1_weight, fc2_weight, depth):
    units, width = fc2_weight.shape
    anywhere = pl.BlockSpec(memory_space=pl.ANY)
    return pl.pallas_call(
        piece_kernel,
        out_shape=jax.ShapeDtypeStruct((depth, width), jnp.bfloat16),
        in_specs=[pl.BlockSpec(memory_space=pltpu.SMEM), anywhere, anywhere],
        out_specs=pl.BlockSpec(memory_space=pltpu.VMEM),
        scratch_shapes=[
            pltpu.VMEM((width, 256), jnp.bfloat16),
            pltpu.VMEM((64, width), jnp.bfloat16),
            pltpu.SemaphoreType.DMA,
        ],
        compiler_params=pltpu.CompilerParams(vmem_limit_bytes=50 * 1024 * 1024),
    )(mine[None], fc1_weight, fc2_weight)


def away_kernel(rows_ref, part_ref, bias_ref, fetched_ref, out_ref, w1, w2, hidden, sems):
    units, width = w1.shape
    parts = []
    for at in range(0, units, 256):
        span = pl.ds(at, min(256, units - at))
        parts.append((span, fetched_ref.at[span], w1.at[span]))
    firsts = len(parts)
    for at in range(0, width, 640):
        span = pl.ds(at, min(640, width - at))
        parts.append((span, fetched_ref.at[pl.ds(units, units), span], w2.at[:, span]))
    copies = [
        pltpu.make_async_copy(source, held, sems.at[i]) for i, (_, source, held) in enumerate(parts)
    ]
    copies[0].start()
    copies[1].start()
    for i, (span, _, _) in enumerate(parts):
        copies[i].wait()
        if i + 2 < len(parts):
            copies[i + 2].start()
        if i < firsts:
            pre = lax.dot_general(
                rows_ref[...], w1[span], (((1,), (1,)), ((), ())), preferred_element_type=jnp.float32
            ) + bias_ref[:, span]
            hidden[:, span] = (0.5 * pre * (1.0 + lax.erf(pre * np.float32(0.5**0.5)))).astype(jnp.bfloat16)
        else:
            out = jnp.dot(hidden[...], w2[:, span], preferred_element_type=jnp.float32)
            out_ref[:, span] = (part_ref[:, span] + out).astype(jnp.bfloat16)


def add_away(rows, part, bias, fetched):
    count, width = rows.shape
    units = bias.shape[0]
    vmem = pl.BlockSpec(memory_space=pltpu.VMEM)
    return pl.pallas_call(
        away_kernel,
        out_shape=jax.ShapeDtypeStruct((count, width), jnp.bfloat16),
        in_specs=[vmem, vmem, vmem, pl.BlockSpec(memory_space=pl.ANY)],
        out_specs=vmem,
        scratch_shapes=[
            pltpu.VMEM((units, width), jnp.bfloat16),
            pltpu.VMEM((units, width), jnp.bfloat16),
            pltpu.VMEM((count, units), jnp.bfloat16),
            pltpu.SemaphoreType.DMA((-(-units // 256) - (-width // 640),)),
        ],
        compiler_params=pltpu.CompilerParams(vmem_limit_bytes=46 * 1024 * 1024),
    )(rows, part, bias[None], fetched)


def pick(chosen, rows):
    return jnp.dot(chosen, rows, preferred_element_type=jnp.float32).astype(jnp.bfloat16)


def per_device(
    patches, live, rounds, ln_gain, fc1_weight, fc1_bias, fc2_weight, fc2_bias, layer_scale
):
    sections = lax.axis_size("section")
    dps = lax.axis_size("dp")
    mine = lax.axis_index("section").astype(jnp.int32)
    keep = 3 * sections // 8
    groups = half_groups(sections)
    width, units = fc1_weight.shape
    f32 = jnp.float32

    def send(value, hops):
        return lax.ppermute(value, AXES, shift_pairs(sections, dps, hops))

    pieces = sections // 4
    depth = units // pieces
    piece = cut_piece(mine, fc1_weight, fc2_weight, depth)
    piece, live = lax.optimization_barrier((piece, live))
    rows, pick_far, pick_near = plan(patches[0], live, rounds, mine, keep)
    piece = lax.ppermute(piece, AXES, opposite_pairs(sections, dps, dps // 2))
    rows = lax.cond(
        live[0, 0] > 0,
        lambda rows: lax.all_to_all(
            rows, "section", split_axis=0, concat_axis=0, axis_index_groups=groups, tiled=True
        ),
        jnp.zeros_like,
        rows,
    )
    piece = lax.optimization_barrier((piece, rows))[0]
    fetched = lax.all_gather(piece, "section", axis=0, axis_index_groups=groups, tiled=True)
    crossing = pick(pick_far, rows)
    bias = lax.optimization_barrier((fc1_bias, crossing))[0]
    away_bias = send(bias, dps // 2)
    crossed, away_bias = lax.optimization_barrier((send(crossing, dps), away_bias))
    routed = pick(pick_near, rows) + crossed

    rows32 = routed.astype(f32)
    mean = jnp.mean(rows32, axis=1, keepdims=True)
    centered = rows32 - mean
    var = jnp.mean(centered * centered, axis=1, keepdims=True)
    normed = (centered * lax.rsqrt(var + 1e-06) * ln_gain).astype(jnp.bfloat16)

    up2, down2 = send(normed, 2), send(normed, -2)
    up13 = send(jnp.concatenate([normed, up2], axis=0), 1)
    down13 = send(jnp.concatenate([normed, down2], axis=0), -1)
    up4 = send(up2, 2)
    blocks = jnp.concatenate([up13, up2, up4, down13, down2, normed], axis=0)

    pre = jnp.dot(blocks, fc1_weight, preferred_element_type=f32) + fc1_bias
    hidden = jax.nn.gelu(pre, approximate=False).astype(jnp.bfloat16)
    part = jnp.dot(hidden, fc2_weight, preferred_element_type=f32)
    part = add_away(blocks, part, away_bias, fetched)

    def add(*parts):
        return sum(p.astype(f32) for p in parts)

    up02 = send(part[: 2 * keep], -1)
    up_far = send(part[3 * keep : 4 * keep], -2)
    down02 = send(part[4 * keep : 6 * keep], 1)
    up_sum = add(part[2 * keep : 3 * keep], up02[keep:], up_far).astype(jnp.bfloat16)
    down_sum = add(part[6 * keep : 7 * keep], down02[keep:]).astype(jnp.bfloat16)
    summed = add(send(up_sum, -2), up02[:keep], send(down_sum, 2), down02[:keep], part[7 * keep :])
    encoded = (rows32 + layer_scale * (summed + fc2_bias)).astype(jnp.bfloat16)
    return encoded[None]


def solution(mesh):
    placed = (
        P("dp", "section", None),
        P("dp", None),
        P("dp", None),
        P(),
        P(None, "dp"),
        P("dp"),
        P("dp", None),
        P(),
        P(),
    )
    return jax.shard_map(
        per_device, mesh=mesh, in_specs=placed, out_specs=P("dp", "section", None), check_vma=False
    )
```
